128 devices in a mesh: ctx: 32 (over z, x_hi, y), head: 4 (over x_lo, core).
Axes of the slice: x: 4 (x_hi: 2, x_lo: 2; x = x_hi * 2 + x_lo), y: 4, z: 4, core: 2. Of those that a mesh axis runs over, the one named last changes fastest.
Arguments:
- queries: bfloat16 [16384, 4096], P('ctx', 'head'), may hold values from -140 to 140
- keys: bfloat16 [16384, 1024], P('ctx', 'head'), may hold values from -10 to 10
- values: bfloat16 [16384, 1024], P('ctx', 'head'), may hold values from -6 to 6
- selected: int32 [32, 3], P('ctx'), may hold values from 0 to 31, as said below
- out_weight: bfloat16 [4096, 4096], P('head'), may hold values from -0.09375 to 0.09375
- out_grad: bfloat16 [16384, 4096], P('ctx', 'head'), may hold values from -6 to 6
Outputs:
- projected: bfloat16 [16384, 4096], P('ctx', 'head')
- query_grad: bfloat16 [16384, 4096], P('ctx', 'head')
- key_grad: bfloat16 [16384, 1024], P('ctx', 'head')
- value_grad: bfloat16 [16384, 1024], P('ctx', 'head')
The draws below stay inside these ranges and needn't reach their ends.
Inputs may be any that keep to these rules, and one draw needn't show every extreme that they name: selected[b, 0] = b. Each other entry is either b (an unused slot) or a distinct earlier block at most 4 blocks before b.
All inputs are finite; a program needn't handle non-finite values.
Results may differ from the reference program's by a relative error of at most 0.034.
Values may be sent and summed in bfloat16 or wider, within the bound.
A program may use at most 192 MiB of HBM per device.

```python
import math
import jax
import jax.numpy as jnp
from jax import lax

D = 4096
HQ = 32
HK = 8
HD = 128
BLOCK = 512
TOPK = 3
CYCLE = 4
BLK_DEV = 1
TOKENS = 16384
N_CTX = 32
N_HEAD = 4


def shared_drawn(key):
    drawn = jax.random.normal(key, (TOKENS // BLOCK, BLOCK, HK, HD), jnp.float32)
    return jnp.clip(drawn, -4.5, 4.5)


def draw_keys(key, part):
    drawn = shared_drawn(key)
    key = jax.random.fold_in(key, 11)
    row_scale = jnp.exp(jax.random.uniform(key, (TOKENS // BLOCK, BLOCK, 1, 1), jnp.float32, math.log(0.5), math.log(2.0)))
    scaled = drawn * row_scale
    return scaled.reshape(TOKENS, HK * HD).astype(jnp.bfloat16)


def draw_queries(key, part):
    key = jax.random.fold_in(key, 23)
    group_size = HQ // HK
    shape = (TOKENS // BLOCK, BLOCK, HK, group_size, HD)
    row_scale = jnp.exp(jax.random.uniform(jax.random.fold_in(key, 3), (TOKENS // BLOCK, BLOCK, 1, 1, 1), jnp.float32, math.log(0.3), math.log(3.0)))
    other = jnp.clip(jax.random.normal(key, shape, jnp.float32), -4.5, 4.5)
    scaled = other * row_scale
    return scaled.reshape(TOKENS, HQ * HD).astype(jnp.bfloat16)


def draw_selected(key, part):
    key = jax.random.fold_in(key, 37)
    block_total = BLK_DEV * N_CTX
    span = CYCLE * BLK_DEV
    ranking = jax.random.randint(key, (block_total, span), 0, 1 << 20) * span + jnp.arange(span)[None, :]
    order = jnp.argsort(ranking, axis=1)
    distance = order[:, :TOPK - 1] + 1
    blocks = jnp.arange(block_total)[:, None]
    earlier = blocks - distance
    others = jnp.where(earlier >= 0, earlier, blocks)
    return jnp.concatenate([blocks, others], axis=1).astype(jnp.int32)


def level_of(rng, shape, split, smallest, largest):
    def one(dim, blocks):
        heights = jax.random.uniform(jax.random.fold_in(jax.random.fold_in(rng, 6), dim), (blocks,), jnp.float32, smallest / len(split), largest / len(split))
        return jnp.repeat(jnp.exp(heights), shape[dim] // blocks).reshape((-1,) + (1,) * (len(shape) - dim - 1))

    loudness = one(*split[0])
    for cut in split[1:]:
        loudness = loudness * one(*cut)
    return loudness


def scatter_about(own_key, shape, scale, limit, shards=(), held_as=jnp.bfloat16):
    gain = level_of(own_key, shape, shards, -0.22, 0.18) if shards else 1.0
    result = jax.random.normal(own_key, shape, jnp.float32) * scale * gain
    return jnp.minimum(jnp.maximum(result, -limit), limit).astype(held_as)


def setup_inputs(seed: int = 0) -> dict:
    key_of = jax.random.split(jax.random.key(seed), 7)
    queries = draw_queries(jax.random.fold_in(key_of[6], 71), 0)
    keys = draw_keys(jax.random.fold_in(key_of[6], 71), 0)
    values = scatter_about(key_of[2], (TOKENS, HK * HD), 1.0, 6.0, ((0, 32), (1, 4)))
    selected = draw_selected(jax.random.fold_in(key_of[6], 71), 0)
    out_weight = scatter_about(key_of[4], (HQ * HD, D), (HQ * HD) ** -0.5, 0.09375, ((0, 4),))
    out_grad = scatter_about(key_of[5], (TOKENS, D), 1.0, 6.0, ((0, 32), (1, 4)))
    return {"queries": queries, "keys": keys, "values": values, "selected": selected, "out_weight": out_weight, "out_grad": out_grad}


def reference(queries, keys, values, selected, out_weight, out_grad):
    score_scale = 1.0 / math.sqrt(HD)
    block_total = selected.shape[0]
    group_size = HQ // HK
    query_tiles = queries.reshape(block_total, BLOCK, HK, group_size, HD)
    key_blocks = keys.reshape(block_total, BLOCK, HK, HD)
    value_blocks = values.reshape(block_total, BLOCK, HK, HD)
    attn_grad = jnp.dot(out_grad, out_weight.T, preferred_element_type=jnp.float32).astype(jnp.bfloat16)
    grad_tiles = attn_grad.reshape(block_total, BLOCK, HK, group_size, HD)
    positions = jnp.arange(BLOCK)
    causal = positions[None, :] <= positions[:, None]
    slot_ids = jnp.arange(TOPK)

    def per_block(block_index):
        chosen = selected[block_index]
        key_tiles = jnp.take(key_blocks, chosen, axis=0).reshape(TOPK * BLOCK, HK, HD).astype(jnp.float32)
        value_tiles = jnp.take(value_blocks, chosen, axis=0).reshape(TOPK * BLOCK, HK, HD).astype(jnp.float32)
        query_tile = query_tiles[block_index].astype(jnp.float32)
        grad_tile = grad_tiles[block_index].astype(jnp.float32)
        live = chosen != block_index
        visible = jnp.where((slot_ids == 0)[:, None, None], causal[None], live[:, None, None])
        visible = visible.transpose(1, 0, 2).reshape(BLOCK, TOPK * BLOCK)
        scores = jnp.einsum('qgrd,kgd->grqk', query_tile, key_tiles) * score_scale
        scores = jnp.where(visible, scores, -1e+30)
        highest = lax.optimization_barrier(jnp.max(scores, axis=-1, keepdims=True))
        expo = jnp.exp(scores - highest)
        weights = expo / lax.optimization_barrier(jnp.sum(expo, axis=-1, keepdims=True))
        weights_half = lax.optimization_barrier(weights.astype(jnp.bfloat16)).astype(jnp.float32)
        attn_tile = jnp.einsum('grqk,kgd->qgrd', weights_half, value_tiles).astype(jnp.bfloat16)
        row_dot = jnp.einsum('qgrd,qgrd->grq', grad_tile, attn_tile.astype(jnp.float32))
        grad_prob = jnp.einsum('qgrd,kgd->grqk', grad_tile, value_tiles)
        grad_score = weights * (grad_prob - row_dot[..., None])
        grad_score = lax.optimization_barrier(grad_score.astype(jnp.bfloat16)).astype(jnp.float32)
        query_grad = (jnp.einsum('grqk,kgd->qgrd', grad_score, key_tiles) * score_scale).astype(jnp.bfloat16)
        key_part = jnp.einsum('grqk,qgrd->kgd', grad_score, query_tile) * score_scale
        value_part = jnp.einsum('grqk,qgrd->kgd', weights_half, grad_tile)
        return (attn_tile, query_grad, key_part.reshape(TOPK, BLOCK, HK * HD), value_part.reshape(TOPK, BLOCK, HK * HD))
    attn_tiles, query_grads, key_parts, value_parts = lax.map(per_block, jnp.arange(block_total))
    flat_index = selected.reshape(-1).astype(jnp.int32)
    key_grad = jnp.zeros((block_total, BLOCK, HK * HD), jnp.float32).at[flat_index].add(key_parts.reshape(block_total * TOPK, BLOCK, HK * HD))
    value_grad = jnp.zeros((block_total, BLOCK, HK * HD), jnp.float32).at[flat_index].add(value_parts.reshape(block_total * TOPK, BLOCK, HK * HD))
    attn_all = attn_tiles.reshape(TOKENS, HQ * HD)
    group_width = HQ * HD // N_HEAD
    projected = jnp.zeros((TOKENS, D), jnp.float32)
    for group_index in range(N_HEAD):
        lower = group_index * group_width
        term = jnp.dot(attn_all[:, lower:lower + group_width], out_weight[lower:lower + group_width], preferred_element_type=jnp.float32)
        projected = projected + lax.optimization_barrier(term.astype(jnp.bfloat16)).astype(jnp.float32)
    return (projected.astype(jnp.bfloat16), query_grads.reshape(TOKENS, HQ * HD), key_grad.reshape(TOKENS, HK * HD).astype(jnp.bfloat16), value_grad.reshape(TOKENS, HK * HD).astype(jnp.bfloat16))
```

```python
import functools
import math

import jax
import jax.numpy as jnp
from jax import lax
from jax.experimental import pallas as pl
from jax.experimental.pallas import tpu as pltpu
from jax.sharding import PartitionSpec as P

HD = 128
BLOCK = 512
HALF = BLOCK // 2
WIDTH = 1024
GROUP = 4
KV = 2
ROW = 4
MESH = pl.DeviceIdType.MESH
SCALE = 1.0 / math.sqrt(HD)
EXP2_SCALE = SCALE * math.log2(math.e)
BF16 = jnp.bfloat16
F32 = jnp.float32
OG_CUTS = 2
OG_ROWS = BLOCK // OG_CUTS


def nn(a, b):
    return lax.dot_general(a, b, (((1,), (0,)), ((), ())), preferred_element_type=F32)


def nt(a, b):
    return lax.dot_general(a, b, (((1,), (1,)), ((), ())), preferred_element_type=F32)


def kernel(
    sel, q_hbm, k_hbm, v_hbm, w_hbm, og_hbm,
    proj_hbm, dq_hbm, dk_hbm, dv_hbm,
    own, win0, win1, vt, kt, qv, wv, ogb, dot_, ot, ob, rl, eb, sb, acc,
    gs0, gs1, gr0, gr1, gxs, gxr, pcs, pcr, pxs, pxr, pown, dqv, dkv_out,
    lsem, osem, xs, xr, ds_, dr, ocs, ocr, oxs, oxr, ofs, ofr, pcss, pcrs, pxss, pxrs, bds, bdr, bxs, bxr,
):
    win = (win0, win1)
    gs = (gs0, gs1)
    gr = (gr0, gr1)
    ctx = lax.axis_index("ctx")
    head = lax.axis_index("head")
    y = lax.rem(ctx, ROW)
    row_start = ctx - y
    following = lax.rem(ctx + ROW, 32)
    preceding = lax.rem(ctx + 32 - ROW, 32)
    chip = head // 2
    core = lax.rem(head, 2)
    other_core = chip * 2 + 1 - core
    other_chip = (1 - chip) * 2 + core
    diagonal = (1 - chip) * 2 + 1 - core

    def peer(k):
        return row_start + lax.rem(y + k, ROW)

    def remote(src, dst, ss, rs, c, h):
        return pltpu.make_async_remote_copy(
            src_ref=src, dst_ref=dst, send_sem=ss, recv_sem=rs, device_id=(c, h), device_id_type=MESH
        )

    kv_in = []
    for g in range(KV):
        cols = pl.ds(g * HD, HD)
        kv_in.append(
            (
                pltpu.make_async_copy(k_hbm.at[:, cols], own.at[g, 0], lsem.at[2 * g]),
                pltpu.make_async_copy(v_hbm.at[:, cols], own.at[g, 1], lsem.at[2 * g + 1]),
            )
        )
        kv_in[g][0].start()
        kv_in[g][1].start()
    og_in = pltpu.make_async_copy(og_hbm, ogb.at[head], lsem.at[4])
    og_in.start()
    w_in = pltpu.make_async_copy(w_hbm, wv, lsem.at[5])
    w_in.start()
    q_in = pltpu.make_async_copy(q_hbm, qv, lsem.at[6])
    q_in.start()

    barrier = pltpu.get_barrier_semaphore()
    for c, h in (
        (following, head), (preceding, head), (peer(1), head), (peer(2), head), (peer(3), head),
        (ctx, other_core), (ctx, other_chip),
    ):
        pl.semaphore_signal(barrier, inc=1, device_id=(c, h), device_id_type=MESH)
    pl.semaphore_wait(barrier, 7)

    cross = [
        remote(own.at[g], win[g].at[y], xs.at[g], xr.at[g], following, head) for g in range(KV)
    ]
    serve_own = [
        [remote(own.at[g], win[g].at[y], ds_.at[g, k - 1], dr.at[g, k - 1], peer(k), head) for k in (1, 2, 3)]
        for g in range(KV)
    ]
    serve_prev = [
        [remote(win[g].at[y], win[g].at[y], ds_.at[g, k - 1], dr.at[g, k - 1], peer(k), head) for k in (1, 2, 3)]
        for g in range(KV)
    ]
    for g in range(KV):
        kv_in[g][0].wait()
        kv_in[g][1].wait()
        cross[g].start()
        for k in (1, 3, 2):
            pl.when(y + k < ROW)(serve_own[g][k - 1].start)

    og_in.wait()
    og_core = remote(ogb.at[head], ogb.at[head], ocs.at[0], ocr.at[0], ctx, other_core)
    og_core.start()
    og_chip = []
    og_pass = []
    for i in range(OG_CUTS):
        rows = pl.ds(i * OG_ROWS, OG_ROWS)
        og_chip.append(
            remote(ogb.at[head, rows], ogb.at[head, rows], oxs.at[i], oxr.at[i], ctx, other_chip)
        )
        og_pass.append(
            remote(ogb.at[other_chip, rows], ogb.at[other_chip, rows], ofs.at[i], ofr.at[i], ctx, other_core)
        )

    def grad_block(block, first):
        cols = pl.ds(pl.multiple_of(block * WIDTH, WIDTH), WIDTH)

        def step(i, _):
            rows = pl.ds(pl.multiple_of(i * 256, 256), 256)
            part = nt(wv[rows, cols], ogb[block])
            dot_[rows, :] = part if first else dot_[rows, :] + part
            return 0

        lax.fori_loop(0, WIDTH // 256, step, 0)

    w_in.wait()
    grad_block(head, True)

    for g in range(KV):
        cross[g].wait_recv()
        for k in (3, 1, 2):
            pl.when(y + k >= ROW)(serve_prev[g][k - 1].start)
        og_chip[g].start()
        if g == 0:
            og_core.wait_recv()
            grad_block(other_core, False)

    sel1 = sel[0, 1]
    sel2 = sel[0, 2]
    col1 = lax.rem(sel1, ROW)
    col2 = lax.rem(sel2, ROW)
    live1 = sel1 != ctx
    live2 = sel2 != ctx

    key_pos = lax.broadcasted_iota(jnp.int32, (HALF, BLOCK), 0)
    query_pos = lax.broadcasted_iota(jnp.int32, (HALF, BLOCK), 1)

    def forward(g):
        w_ = win[g]
        vt[0] = own[g, 1].T
        vt[1] = w_[col1, 1].T
        vt[2] = w_[col2, 1].T

        def one_head(r, _):
            hh = g * GROUP + r
            hcols = pl.ds(pl.multiple_of(hh * HD, HD), HD)
            q = qv[:, hcols]
            s = nt(own[g, 0, :HALF], q)
            s = jnp.where(key_pos <= query_pos, s, -1e30)
            sb[0:HALF, :] = s
            top = jnp.max(s, axis=0, keepdims=True)
            s = nt(own[g, 0, HALF:], q[HALF:])
            s = jnp.where((key_pos <= query_pos)[:, :HALF], s, -1e30)
            sb[HALF:BLOCK, HALF:] = s
            top = jnp.concatenate(
                [top[:, :HALF], jnp.maximum(top[:, HALF:], jnp.max(s, axis=0, keepdims=True))], axis=1
            )
            for j, (col, live) in enumerate(((col1, live1), (col2, live2))):
                for half in range(2):
                    s = nt(w_[col, 0, half * HALF : (half + 1) * HALF], q)
                    sb[BLOCK * (j + 1) + half * HALF : BLOCK * (j + 1) + (half + 1) * HALF, :] = s
                    top = jnp.maximum(top, jnp.where(live, jnp.max(s, axis=0, keepdims=True), -1e30))
            shift = top * EXP2_SCALE
            e = jnp.exp2(sb[0:HALF, :] * EXP2_SCALE - shift)
            total = jnp.sum(e, axis=0, keepdims=True)
            e = e.astype(BF16)
            eb[hh, 0:HALF, :] = e
            out = nn(vt[0, :, :HALF], e)
            e = jnp.exp2(sb[HALF:BLOCK, HALF:] * EXP2_SCALE - shift[:, HALF:])
            total = jnp.concatenate(
                [total[:, :HALF], total[:, HALF:] + jnp.sum(e, axis=0, keepdims=True)], axis=1
            )
            e = e.astype(BF16)
            eb[hh, HALF:BLOCK, HALF:] = e
            out2 = nn(vt[0, :, HALF:], e)
            out = jnp.concatenate([out[:, :HALF], out[:, HALF:] + out2], axis=1)
            for j, live in enumerate((live1, live2)):
                sh = jnp.where(live, shift, 1e30)
                for half in range(2):
                    rows = slice(BLOCK * (j + 1) + half * HALF, BLOCK * (j + 1) + (half + 1) * HALF)
                    e = jnp.exp2(sb[rows, :] * EXP2_SCALE - sh)
                    total = total + jnp.sum(e, axis=0, keepdims=True)
                    e = e.astype(BF16)
                    eb[hh, rows, :] = e
                    out = out + nn(vt[j + 1, :, half * HALF : (half + 1) * HALF], e)
            recip = 1.0 / total
            rl[hh] = recip
            out = out * recip
            hrows = pl.ds(pl.multiple_of(hh * HD, HD), HD)
            ot[hrows, :] = out
            ob[:, hcols] = out.T.astype(BF16)
            return 0

        lax.fori_loop(0, GROUP, one_head, 0)

    for g in range(KV):
        if g == 0:
            q_in.wait()
        for k in (1, 2, 3):
            serve_own[g][k - 1].wait_recv()
        forward(g)
        og_chip[g].wait_recv()
        og_pass[g].start()

    def project(block, put):
        def step(i, _):
            n0 = pl.multiple_of(i * 256, 256)
            cols = pl.ds(pl.multiple_of(block * WIDTH + n0, 256), 256)
            put(pl.ds(n0, 256), nn(ob[...], wv[:, cols]))
            return 0

        lax.fori_loop(0, WIDTH // 256, step, 0)

    def to_core(slot):
        def put(cols, val):
            pcs[slot, :, cols] = val.astype(BF16)

        return put

    def to_chip(cols, val):
        pxs[:, cols] = val.astype(BF16)

    def keep(cols, val):
        pown[:, cols] = val

    p_core = [remote(pcs.at[i], pcr.at[i], pcss.at[i], pcrs.at[i], ctx, other_core) for i in range(2)]
    p_chip = remote(pxs, pxr, pxss.at[0], pxrs.at[0], ctx, other_chip)
    project(diagonal, to_core(0))
    p_core[0].start()
    project(other_chip, to_chip)
    p_core[0].wait_recv()
    pxs[...] = (pxs[...].astype(F32) + pcr[0].astype(F32)).astype(BF16)
    p_chip.start()
    project(other_core, to_core(1))
    p_core[1].start()
    project(head, keep)

    for i in range(OG_CUTS):
        og_pass[i].wait_recv()
    grad_block(other_chip, False)
    grad_block(diagonal, False)

    def backward(g, start, stop):
        w_ = win[g]
        if start == 0:
            kt[0] = own[g, 0].T
            kt[1] = w_[col1, 0].T
            kt[2] = w_[col2, 0].T
            acc[g] = jnp.zeros(acc.shape[1:], F32)

        def one_head(r, _):
            hh = g * GROUP + r
            hcols = pl.ds(pl.multiple_of(hh * HD, HD), HD)
            hrows = pl.ds(pl.multiple_of(hh * HD, HD), HD)
            q = qv[:, hcols]
            do32 = dot_[hrows, :] * rl[hh]
            do = do32.astype(BF16)
            rd = jnp.sum(do32 * ot[hrows, :], axis=0, keepdims=True)
            e = eb[hh, 0:HALF, :]
            dp = nn(own[g, 1, :HALF], do)
            dsv = (e.astype(F32) * (dp - rd)).astype(BF16)
            acc[g, 1, 0, :HALF] += nt(e, do)
            acc[g, 0, 0, :HALF] += nn(dsv, q)
            dqt = nn(kt[0, :, :HALF], dsv)
            e = eb[hh, HALF:BLOCK, HALF:]
            dp = nn(own[g, 1, HALF:], do[:, HALF:])
            dsv = (e.astype(F32) * (dp - rd[:, HALF:])).astype(BF16)
            acc[g, 1, 0, HALF:] += nt(e, do[:, HALF:])
            acc[g, 0, 0, HALF:] += nn(dsv, q[HALF:])
            dqt2 = nn(kt[0, :, HALF:], dsv)
            dqt = jnp.concatenate([dqt[:, :HALF], dqt[:, HALF:] + dqt2], axis=1)
            for j, col in enumerate((col1, col2)):
                for half in range(2):
                    part = slice(half * HALF, (half + 1) * HALF)
                    rows = slice(BLOCK * (j + 1) + half * HALF, BLOCK * (j + 1) + (half + 1) * HALF)
                    e = eb[hh, rows, :]
                    dp = nn(w_[col, 1, part], do)
                    dsv = (e.astype(F32) * (dp - rd)).astype(BF16)
                    acc[g, 1, j + 1, part] += nt(e, do)
                    acc[g, 0, j + 1, part] += nn(dsv, q)
                    dqt = dqt + nn(kt[j + 1, :, part], dsv)
            dqv[:, hcols] = (dqt * SCALE).T.astype(BF16)
            return 0

        lax.fori_loop(start, stop, one_head, 0)

    give = [
        [
            remote(
                gs[g].at[lax.rem(y + ROW - k, ROW)], gr[g].at[k - 1], bds.at[g, k - 1], bdr.at[g, k - 1],
                row_start + lax.rem(y + ROW - k, ROW), head,
            )
            for k in (1, 2, 3)
        ]
        for g in range(KV)
    ]
    give_back = [remote(gxs.at[g], gxr.at[g], bxs.at[g], bxr.at[g], preceding, head) for g in range(KV)]

    def send_grads(g):
        for part in range(2):
            factor = SCALE if part == 0 else 1.0
            one = acc[g, part, 1] * factor
            two = acc[g, part, 2] * factor
            for c in range(ROW):
                gs[g][c, part] = (jnp.where(col1 == c, one, 0.0) + jnp.where(col2 == c, two, 0.0)).astype(BF16)
        for k in (1, 3, 2):
            give[g][k - 1].start()

    def sum_grads(g):
        for k in (1, 2, 3):
            give[g][k - 1].wait_recv()
        for part in range(2):
            factor = SCALE if part == 0 else 1.0
            mine = acc[g, part, 0] * factor
            back = gs[g][y, part].astype(F32)
            for k in (1, 2, 3):
                came = gr[g][k - 1, part].astype(F32)
                inside = y + k < ROW
                mine = mine + jnp.where(inside, came, 0.0)
                back = back + jnp.where(inside, 0.0, came)
            acc[g, part, 0] = mine
            gxs[g, part] = back.astype(BF16)
        give_back[g].start()

    outs = []

    def finish_grads(g):
        give_back[g].wait_recv()
        for part in range(2):
            dkv_out[g, part] = (acc[g, part, 0] + gxr[g, part].astype(F32)).astype(BF16)
        for part, ref in ((0, dk_hbm), (1, dv_hbm)):
            cp = pltpu.make_async_copy(dkv_out.at[g, part], ref.at[:, pl.ds(g * HD, HD)], osem.at[2 * g + part])
            cp.start()
            outs.append(cp)

    backward(0, 0, GROUP)
    send_grads(0)
    backward(1, 0, 2)
    sum_grads(0)
    backward(1, 2, GROUP)
    send_grads(1)
    cp = pltpu.make_async_copy(dqv, dq_hbm, osem.at[4])
    cp.start()
    outs.append(cp)
    finish_grads(0)
    p_core[1].wait_recv()
    p_chip.wait_recv()
    pown[...] = pown[...] + pcr[1].astype(F32) + pxr[...].astype(F32)
    pxs_done = p_chip
    pxs_done.wait_send()
    pxs[...] = pown[...].astype(BF16)
    cp = pltpu.make_async_copy(pxs, proj_hbm, osem.at[5])
    cp.start()
    outs.append(cp)
    sum_grads(1)
    finish_grads(1)

    og_core.wait_send()
    for i in range(OG_CUTS):
        og_chip[i].wait_send()
        og_pass[i].wait_send()
    for i in range(2):
        p_core[i].wait_send()
    for g in range(KV):
        cross[g].wait_send()
        give_back[g].wait_send()
        for k in (1, 2, 3):
            serve_own[g][k - 1].wait_send()
            give[g][k - 1].wait_send()
    for cp in outs:
        cp.wait()


def local(queries, keys, values, selected, out_weight, out_grad):
    vm = pltpu.VMEM
    dma = pltpu.SemaphoreType.DMA
    anyspec = pl.BlockSpec(memory_space=pl.ANY)
    return pl.pallas_call(
        kernel,
        out_shape=(
            jax.ShapeDtypeStruct((BLOCK, WIDTH), BF16),
            jax.ShapeDtypeStruct((BLOCK, WIDTH), BF16),
            jax.ShapeDtypeStruct((BLOCK, KV * HD), BF16),
            jax.ShapeDtypeStruct((BLOCK, KV * HD), BF16),
        ),
        in_specs=[pl.BlockSpec(memory_space=pltpu.SMEM)] + [anyspec] * 5,
        out_specs=(anyspec,) * 4,
        scratch_shapes=[
            vm((KV, 2, BLOCK, HD), BF16),
            vm((ROW, 2, BLOCK, HD), BF16),
            vm((ROW, 2, BLOCK, HD), BF16),
            vm((3, HD, BLOCK), BF16),
            vm((3, HD, BLOCK), BF16),
            vm((BLOCK, WIDTH), BF16),
            vm((WIDTH, 4 * WIDTH), BF16),
            vm((4, BLOCK, WIDTH), BF16),
            vm((WIDTH, BLOCK), F32),
            vm((WIDTH, BLOCK), F32),
            vm((BLOCK, WIDTH), BF16),
            vm((KV * GROUP, 1, BLOCK), F32),
            vm((KV * GROUP, 3 * BLOCK, BLOCK), BF16),
            vm((3 * BLOCK, BLOCK), F32),
            vm((KV, 2, 3, BLOCK, HD), F32),
            vm((ROW, 2, BLOCK, HD), BF16),
            vm((ROW, 2, BLOCK, HD), BF16),
            vm((3, 2, BLOCK, HD), BF16),
            vm((3, 2, BLOCK, HD), BF16),
            vm((KV, 2, BLOCK, HD), BF16),
            vm((KV, 2, BLOCK, HD), BF16),
            vm((2, BLOCK, WIDTH), BF16),
            vm((2, BLOCK, WIDTH), BF16),
            vm((BLOCK, WIDTH), BF16),
            vm((BLOCK, WIDTH), BF16),
            vm((BLOCK, WIDTH), F32),
            vm((BLOCK, WIDTH), BF16),
            vm((KV, 2, BLOCK, HD), BF16),
            dma((7,)), dma((6,)),
            dma((KV,)), dma((KV,)), dma((KV, 3)), dma((KV, 3)),
            dma((1,)), dma((1,)), dma((OG_CUTS,)), dma((OG_CUTS,)), dma((OG_CUTS,)), dma((OG_CUTS,)),
            dma((2,)), dma((2,)), dma((1,)), dma((1,)),
            dma((KV, 3)), dma((KV, 3)), dma((KV,)), dma((KV,)),
        ],
        compiler_params=pltpu.CompilerParams(
            collective_id=0, has_side_effects=True, vmem_limit_bytes=63 * 1024 * 1024
        ),
        cost_estimate=pl.CostEstimate(flops=18 * 10**9, bytes_accessed=16 * 2**20, transcendentals=6 * 10**6),
        name="layer",
    )(selected, queries, keys, values, out_weight, out_grad)


def solution(mesh):
    placed = (
        P("ctx", "head"),
        P("ctx", "head"),
        P("ctx", "head"),
        P("ctx", None),
        P("head", None),
        P("ctx", "head"),
    )
    return jax.shard_map(
        local,
        mesh=mesh,
        in_specs=placed,
        out_specs=(P("ctx", "head"), P("ctx", "head"), P("ctx", "head"), P("ctx", "head")),
        check_vma=False,
    )
```

```python
import functools
import math

import jax
import jax.numpy as jnp
from jax import lax
from jax.experimental import pallas as pl
from jax.experimental.pallas import tpu as pltpu
from jax.sharding import PartitionSpec as P

HD = 128
BLOCK = 512
HALF = BLOCK // 2
WIDTH = 1024
GROUP = 4
KV = 2
ROW = 4
MESH = pl.DeviceIdType.MESH
SCALE = 1.0 / math.sqrt(HD)
EXP2_SCALE = SCALE * math.log2(math.e)
BF16 = jnp.bfloat16
F32 = jnp.float32
OG_CUTS = 2
OG_ROWS = BLOCK // OG_CUTS
CUTS = 2
CUT = WIDTH // CUTS
MOVES = [(n, i * 128, 128) for n in (0, 1) for i in range(4)] + [(n, i * 256, 256) for n in (2, 3) for i in range(2)]


def nn(a, b):
    return lax.dot_general(a, b, (((1,), (0,)), ((), ())), preferred_element_type=F32)


def nt(a, b):
    return lax.dot_general(a, b, (((1,), (1,)), ((), ())), preferred_element_type=F32)


def kernel(
    sel, q_hbm, k_hbm, v_hbm, w_hbm, og_hbm,
    proj_hbm, dq_hbm, dk_hbm, dv_hbm,
    own, win0, win1, vt, kt, qv, wv, ogb, dot_, ot, ob, rl, eb, sb, acc,
    gs0, gs1, gr0, gr1, gxs, gxr, pcs, pcr, pxs, pxr, pown, dqv, dkv_out, dob, rdb,
    lsem, osem, xs, xr, ds_, dr, ocs, ocr, oxs, oxr, ofs, ofr, pcss, pcrs, pxss, pxrs, bds, bdr, bxs, bxr,
):
    win = (win0, win1)
    gs = (gs0, gs1)
    gr = (gr0, gr1)
    ctx = lax.axis_index("ctx")
    head = lax.axis_index("head")
    y = lax.rem(ctx, ROW)
    row_start = ctx - y
    following = lax.rem(ctx + ROW, 32)
    preceding = lax.rem(ctx + 32 - ROW, 32)
    chip = head // 2
    core = lax.rem(head, 2)
    other_core = chip * 2 + 1 - core
    other_chip = (1 - chip) * 2 + core
    diagonal = (1 - chip) * 2 + 1 - core

    def peer(k):
        return row_start + lax.rem(y + k, ROW)

    def remote(src, dst, ss, rs, c, h):
        return pltpu.make_async_remote_copy(
            src_ref=src, dst_ref=dst, send_sem=ss, recv_sem=rs, device_id=(c, h), device_id_type=MESH
        )

    kv_in = []
    for g in range(KV):
        cols = pl.ds(g * HD, HD)
        kv_in.append(
            (
                pltpu.make_async_copy(k_hbm.at[:, cols], own.at[g, 0], lsem.at[2 * g]),
                pltpu.make_async_copy(v_hbm.at[:, cols], own.at[g, 1], lsem.at[2 * g + 1]),
            )
        )
        kv_in[g][0].start()
        kv_in[g][1].start()
    og_in = pltpu.make_async_copy(og_hbm, ogb.at[head], lsem.at[4])
    og_in.start()
    w_in = pltpu.make_async_copy(w_hbm, wv, lsem.at[5])
    w_in.start()
    q_in = pltpu.make_async_copy(q_hbm, qv, lsem.at[6])
    q_in.start()

    barrier = pltpu.get_barrier_semaphore()
    for c, h in (
        (following, head), (preceding, head), (peer(1), head), (peer(2), head), (peer(3), head),
        (ctx, other_core), (ctx, other_chip),
    ):
        pl.semaphore_signal(barrier, inc=1, device_id=(c, h), device_id_type=MESH)
    pl.semaphore_wait(barrier, 7)

    cross = [
        remote(own.at[g], win[g].at[y], xs.at[g], xr.at[g], following, head) for g in range(KV)
    ]
    serve_own = [
        [remote(own.at[g], win[g].at[y], ds_.at[g, k - 1], dr.at[g, k - 1], peer(k), head) for k in (1, 2, 3)]
        for g in range(KV)
    ]
    serve_prev = [
        [remote(win[g].at[y], win[g].at[y], ds_.at[g, k - 1], dr.at[g, k - 1], peer(k), head) for k in (1, 2, 3)]
        for g in range(KV)
    ]
    for g in range(KV):
        kv_in[g][0].wait()
        kv_in[g][1].wait()
        cross[g].start()
        if g == 0:
            for k in (1, 3, 2):
                pl.when(y + k < ROW)(serve_own[g][k - 1].start)

    og_in.wait()
    og_core = remote(ogb.at[head], ogb.at[head], ocs.at[0], ocr.at[0], ctx, other_core)
    og_core.start()
    og_chip = []
    og_pass = []
    for i in range(OG_CUTS):
        rows = pl.ds(i * OG_ROWS, OG_ROWS)
        og_chip.append(
            remote(ogb.at[head, rows], ogb.at[head, rows], oxs.at[i], oxr.at[i], ctx, other_chip)
        )
        og_pass.append(
            remote(ogb.at[other_chip, rows], ogb.at[other_chip, rows], ofs.at[i], ofr.at[i], ctx, other_core)
        )

    def grad_block(block, first):
        cols = pl.ds(pl.multiple_of(block * WIDTH, WIDTH), WIDTH)

        def step(i, _):
            rows = pl.ds(pl.multiple_of(i * 256, 256), 256)
            part = nt(wv[rows, cols], ogb[block])
            dot_[rows, :] = part if first else dot_[rows, :] + part
            return 0

        lax.fori_loop(0, WIDTH // 256, step, 0)

    w_in.wait()
    grad_block(head, True)

    for g in range(KV):
        cross[g].wait_recv()
        for k in (3, 1, 2):
            pl.when(y + k >= ROW)(serve_prev[g][k - 1].start)
        if g == 0:
            for k in (1, 3, 2):
                pl.when(y + k < ROW)(serve_own[1][k - 1].start)
            og_core.wait_recv()
            grad_block(other_core, False)
        else:
            for i in range(OG_CUTS):
                og_chip[i].start()

    sel1 = sel[0, 1]
    sel2 = sel[0, 2]
    col1 = lax.rem(sel1, ROW)
    col2 = lax.rem(sel2, ROW)
    live1 = sel1 != ctx
    live2 = sel2 != ctx

    key_pos = lax.broadcasted_iota(jnp.int32, (HALF, BLOCK), 0)
    query_pos = lax.broadcasted_iota(jnp.int32, (HALF, BLOCK), 1)

    def forward(g):
        w_ = win[g]
        vt[0] = own[g, 1].T
        vt[1] = w_[col1, 1].T
        vt[2] = w_[col2, 1].T

        def one_head(r, _):
            hh = g * GROUP + r
            hcols = pl.ds(pl.multiple_of(hh * HD, HD), HD)
            q = qv[:, hcols]
            s = nt(own[g, 0, :HALF], q)
            s = jnp.where(key_pos <= query_pos, s, -1e30)
            sb[0:HALF, :] = s
            top = jnp.max(s, axis=0, keepdims=True)
            s = nt(own[g, 0, HALF:], q[HALF:])
            s = jnp.where((key_pos <= query_pos)[:, :HALF], s, -1e30)
            sb[HALF:BLOCK, HALF:] = s
            top = jnp.concatenate(
                [top[:, :HALF], jnp.maximum(top[:, HALF:], jnp.max(s, axis=0, keepdims=True))], axis=1
            )
            for j, (col, live) in enumerate(((col1, live1), (col2, live2))):
                for half in range(2):
                    s = nt(w_[col, 0, half * HALF : (half + 1) * HALF], q)
                    sb[BLOCK * (j + 1) + half * HALF : BLOCK * (j + 1) + (half + 1) * HALF, :] = s
                    top = jnp.maximum(top, jnp.where(live, jnp.max(s, axis=0, keepdims=True), -1e30))
            shift = top * EXP2_SCALE
            e = jnp.exp2(sb[0:HALF, :] * EXP2_SCALE - shift)
            total = jnp.sum(e, axis=0, keepdims=True)
            e = e.astype(BF16)
            eb[hh, 0:HALF, :] = e
            out = nn(vt[0, :, :HALF], e)
            e = jnp.exp2(sb[HALF:BLOCK, HALF:] * EXP2_SCALE - shift[:, HALF:])
            total = jnp.concatenate(
                [total[:, :HALF], total[:, HALF:] + jnp.sum(e, axis=0, keepdims=True)], axis=1
            )
            e = e.astype(BF16)
            eb[hh, HALF:BLOCK, HALF:] = e
            out2 = nn(vt[0, :, HALF:], e)
            out = jnp.concatenate([out[:, :HALF], out[:, HALF:] + out2], axis=1)
            for j, live in enumerate((live1, live2)):
                sh = jnp.where(live, shift, 1e30)
                for half in range(2):
                    rows = slice(BLOCK * (j + 1) + half * HALF, BLOCK * (j + 1) + (half + 1) * HALF)
                    e = jnp.exp2(sb[rows, :] * EXP2_SCALE - sh)
                    total = total + jnp.sum(e, axis=0, keepdims=True)
                    e = e.astype(BF16)
                    eb[hh, rows, :] = e
                    out = out + nn(vt[j + 1, :, half * HALF : (half + 1) * HALF], e)
            recip = 1.0 / total
            rl[hh] = recip
            out = out * recip
            hrows = pl.ds(pl.multiple_of(hh * HD, HD), HD)
            ot[hrows, :] = out
            ob[:, hcols] = out.T.astype(BF16)
            return 0

        lax.fori_loop(0, GROUP, one_head, 0)

    for g in range(KV):
        if g == 0:
            q_in.wait()
        for k in (1, 2, 3):
            serve_own[g][k - 1].wait_recv()
        forward(g)

    def project(block, cut, put):
        def step(i, _):
            n0 = pl.multiple_of(i * 256, 256)
            cols = pl.ds(pl.multiple_of(block * WIDTH + cut * CUT + n0, 256), 256)
            put(pl.ds(n0, 256), nn(ob[...], wv[:, cols]))
            return 0

        lax.fori_loop(0, CUT // 256, step, 0)

    def to_core(slot, cut):
        def put(cols, val):
            pcs[slot, cut, :, cols] = val.astype(BF16)

        return put

    def to_chip(cut):
        def put(cols, val):
            pxs[cut, :, cols] = (val + pcr[0, cut, :, cols].astype(F32)).astype(BF16)

        return put

    def keep(cut):
        def put(cols, val):
            pown[cut, :, cols] = val

        return put

    p_core = [
        [remote(pcs.at[i, j], pcr.at[i, j], pcss.at[i, j], pcrs.at[i, j], ctx, other_core) for j in range(CUTS)]
        for i in range(2)
    ]
    p_chip = [remote(pxs.at[j], pxr.at[j], pxss.at[j], pxrs.at[j], ctx, other_chip) for j in range(CUTS)]
    project(diagonal, 0, to_core(0, 0))
    p_core[0][0].start()
    project(diagonal, 1, to_core(0, 1))
    p_core[0][1].start()
    for j in range(CUTS):
        p_core[0][j].wait_recv()
        project(other_chip, j, to_chip(j))
        p_chip[j].start()
        if j == 0:
            for i in range(OG_CUTS):
                og_chip[i].wait_recv()
                og_pass[i].start()
    grad_block(other_chip, False)
    for i in range(OG_CUTS):
        og_pass[i].wait_recv()
    grad_block(diagonal, False)

    def back_tile(g, slot, w_, col, part, hh, q, do, rd, span):
        keys_at = slice(part * HALF, (part + 1) * HALF)
        e = eb[hh, slot * BLOCK + part * HALF : slot * BLOCK + (part + 1) * HALF, span]
        v = own[g, 1, keys_at] if slot == 0 else w_[col, 1, keys_at]
        dp = nn(v, do)
        dsv = (e.astype(F32) * (dp - rd)).astype(BF16)
        acc[g, 1, slot, keys_at] += nt(e, do)
        acc[g, 0, slot, keys_at] += nn(dsv, q)
        return nn(kt[slot, :, keys_at], dsv)

    def backward_far(g):
        w_ = win[g]
        kt[1] = w_[col1, 0].T
        kt[2] = w_[col2, 0].T
        acc[g] = jnp.zeros(acc.shape[1:], F32)

        def one_head(r, _):
            hh = g * GROUP + r
            hcols = pl.ds(pl.multiple_of(hh * HD, HD), HD)
            q = qv[:, hcols]
            do32 = dot_[hcols, :] * rl[hh]
            do = do32.astype(BF16)
            rd = jnp.sum(do32 * ot[hcols, :], axis=0, keepdims=True)
            dob[hcols, :] = do
            rdb[hh] = rd
            dqt = jnp.zeros((HD, BLOCK), F32)
            for slot, col in ((1, col1), (2, col2)):
                for part in range(2):
                    dqt = dqt + back_tile(g, slot, w_, col, part, hh, q, do, rd, slice(None))
            dot_[hcols, :] = dqt
            return 0

        lax.fori_loop(0, GROUP, one_head, 0)

    def backward_near(g):
        kt[0] = own[g, 0].T

        def one_head(r, _):
            hh = g * GROUP + r
            hcols = pl.ds(pl.multiple_of(hh * HD, HD), HD)
            q = qv[:, hcols]
            do = dob[hcols, :]
            rd = rdb[hh]
            dqt = dot_[hcols, :] + back_tile(g, 0, None, None, 0, hh, q, do, rd, slice(None))
            late = back_tile(g, 0, None, None, 1, hh, q[HALF:], do[:, HALF:], rd[:, HALF:], slice(HALF, BLOCK))
            dqt = jnp.concatenate([dqt[:, :HALF], dqt[:, HALF:] + late], axis=1)
            dqv[:, hcols] = (dqt * SCALE).T.astype(BF16)
            return 0

        lax.fori_loop(0, GROUP, one_head, 0)

    give = [
        [
            [
                remote(
                    gs[g].at[lax.rem(y + ROW - k, ROW), part], gr[g].at[k - 1, part],
                    bds.at[g, part, k - 1], bdr.at[g, part, k - 1],
                    row_start + lax.rem(y + ROW - k, ROW), head,
                )
                for k in (1, 2, 3)
            ]
            for part in range(2)
        ]
        for g in range(KV)
    ]
    give_back = [
        [
            remote(gxs.at[g, part], gxr.at[g, part], bxs.at[g, part], bxr.at[g, part], preceding, head)
            for part in range(2)
        ]
        for g in range(KV)
    ]
    factors = (SCALE, 1.0)

    def send_grads(g, part):
        one = acc[g, part, 1] * factors[part]
        two = acc[g, part, 2] * factors[part]
        for c in range(ROW):
            gs[g][c, part] = (jnp.where(col1 == c, one, 0.0) + jnp.where(col2 == c, two, 0.0)).astype(BF16)
        for k in (1, 3, 2):
            give[g][part][k - 1].start()

    def sum_grads(g, part):
        for k in (1, 2, 3):
            give[g][part][k - 1].wait_recv()
        mine = acc[g, part, 0] * factors[part]
        back = gs[g][y, part].astype(F32)
        for k in (1, 2, 3):
            came = gr[g][k - 1, part].astype(F32)
            inside = y + k < ROW
            mine = mine + jnp.where(inside, came, 0.0)
            back = back + jnp.where(inside, 0.0, came)
        gxs[g, part] = back.astype(BF16)
        give_back[g][part].start()
        acc[g, part, 0] = mine

    outs = []

    def finish_grads(g, part):
        give_back[g][part].wait_recv()
        dkv_out[g, part] = (acc[g, part, 0] + gxr[g, part].astype(F32)).astype(BF16)
        ref = (dk_hbm, dv_hbm)[part]
        cp = pltpu.make_async_copy(dkv_out.at[g, part], ref.at[:, pl.ds(g * HD, HD)], osem.at[2 * g + part])
        cp.start()
        outs.append(cp)

    for g in range(KV):
        backward_far(g)
        for part in (1, 0):
            send_grads(g, part)
    for g in range(KV):
        backward_near(g)
    cp = pltpu.make_async_copy(dqv, dq_hbm, osem.at[4])
    cp.start()
    outs.append(cp)
    for j in range(CUTS):
        project(other_core, j, to_core(1, j))
        p_core[1][j].start()
    for part in (1, 0):
        sum_grads(0, part)
    for j in range(CUTS):
        project(head, j, keep(j))
    sum_grads(1, 1)
    for j in range(CUTS):
        p_core[1][j].wait_recv()
        p_chip[j].wait()
        pxs[j] = (pown[j] + pcr[1, j].astype(F32) + pxr[j].astype(F32)).astype(BF16)
        cp = pltpu.make_async_copy(pxs.at[j], proj_hbm.at[:, pl.ds(j * CUT, CUT)], osem.at[5 + j])
        cp.start()
        outs.append(cp)
    sum_grads(1, 0)
    for g in range(KV):
        for part in (1, 0):
            finish_grads(g, part)

    og_core.wait_send()
    for i in range(OG_CUTS):
        og_chip[i].wait_send()
        og_pass[i].wait_send()
    for i in range(2):
        for j in range(CUTS):
            p_core[i][j].wait_send()
    for g in range(KV):
        cross[g].wait_send()
        for k in (1, 2, 3):
            serve_own[g][k - 1].wait_send()
        for part in range(2):
            give_back[g][part].wait_send()
            for k in (1, 2, 3):
                give[g][part][k - 1].wait_send()
    for cp in outs:
        cp.wait()


def mover(*refs):
    ins, outs, held, sems = refs[:4], refs[4:8], refs[8:12], refs[12]
    copies = []
    for i, (n, first, rows) in enumerate(MOVES):
        at = pl.ds(first, rows)
        copies.append(
            (
                pltpu.make_async_copy(ins[n].at[at], held[n].at[at], sems.at[0, i]),
                pltpu.make_async_copy(held[n].at[at], outs[n].at[at], sems.at[1, i]),
            )
        )
    for come, _ in copies:
        come.start()
    for come, go in copies:
        come.wait()
        go.start()
    for _, go in copies:
        go.wait()


def local(queries, keys, values, selected, out_weight, out_grad):
    vm = pltpu.VMEM
    dma = pltpu.SemaphoreType.DMA
    anyspec = pl.BlockSpec(memory_space=pl.ANY)
    shapes = (
        jax.ShapeDtypeStruct((BLOCK, WIDTH), BF16),
        jax.ShapeDtypeStruct((BLOCK, WIDTH), BF16),
        jax.ShapeDtypeStruct((BLOCK, KV * HD), BF16),
        jax.ShapeDtypeStruct((BLOCK, KV * HD), BF16),
    )
    results = pl.pallas_call(
        kernel,
        out_shape=shapes,
        in_specs=[pl.BlockSpec(memory_space=pltpu.SMEM)] + [anyspec] * 5,
        out_specs=(anyspec,) * 4,
        scratch_shapes=[
            vm((KV, 2, BLOCK, HD), BF16),
            vm((ROW, 2, BLOCK, HD), BF16),
            vm((ROW, 2, BLOCK, HD), BF16),
            vm((3, HD, BLOCK), BF16),
            vm((3, HD, BLOCK), BF16),
            vm((BLOCK, WIDTH), BF16),
            vm((WIDTH, 4 * WIDTH), BF16),
            vm((4, BLOCK, WIDTH), BF16),
            vm((WIDTH, BLOCK), F32),
            vm((WIDTH, BLOCK), F32),
            vm((BLOCK, WIDTH), BF16),
            vm((KV * GROUP, 1, BLOCK), F32),
            vm((KV * GROUP, 3 * BLOCK, BLOCK), BF16),
            vm((3 * BLOCK, BLOCK), F32),
            vm((KV, 2, 3, BLOCK, HD), F32),
            vm((ROW, 2, BLOCK, HD), BF16),
            vm((ROW, 2, BLOCK, HD), BF16),
            vm((3, 2, BLOCK, HD), BF16),
            vm((3, 2, BLOCK, HD), BF16),
            vm((KV, 2, BLOCK, HD), BF16),
            vm((KV, 2, BLOCK, HD), BF16),
            vm((2, CUTS, BLOCK, CUT), BF16),
            vm((2, CUTS, BLOCK, CUT), BF16),
            vm((CUTS, BLOCK, CUT), BF16),
            vm((CUTS, BLOCK, CUT), BF16),
            vm((CUTS, BLOCK, CUT), F32),
            vm((BLOCK, WIDTH), BF16),
            vm((KV, 2, BLOCK, HD), BF16),
            vm((WIDTH, BLOCK), BF16),
            vm((KV * GROUP, 1, BLOCK), F32),
            dma((7,)), dma((5 + CUTS,)),
            dma((KV,)), dma((KV,)), dma((KV, 3)), dma((KV, 3)),
            dma((1,)), dma((1,)), dma((OG_CUTS,)), dma((OG_CUTS,)), dma((OG_CUTS,)), dma((OG_CUTS,)),
            dma((2, CUTS)), dma((2, CUTS)), dma((CUTS,)), dma((CUTS,)),
            dma((KV, 2, 3)), dma((KV, 2, 3)), dma((KV, 2)), dma((KV, 2)),
        ],
        compiler_params=pltpu.CompilerParams(
            collective_id=0, has_side_effects=True, vmem_limit_bytes=63 * 1024 * 1024
        ),
        cost_estimate=pl.CostEstimate(flops=18 * 10**9, bytes_accessed=16 * 2**20, transcendentals=6 * 10**6),
        name="layer",
    )(selected, queries, keys, values, out_weight, out_grad)
    return pl.pallas_call(
        mover,
        out_shape=shapes,
        in_specs=[anyspec] * 4,
        out_specs=(anyspec,) * 4,
        scratch_shapes=[vm(x.shape, x.dtype) for x in shapes] + [dma((2, len(MOVES)))],
        compiler_params=pltpu.CompilerParams(vmem_limit_bytes=60 * 1024 * 1024),
        name="move",
    )(*results)


def solution(mesh):
    placed = (
        P("ctx", "head"),
        P("ctx", "head"),
        P("ctx", "head"),
        P("ctx", None),
        P("head", None),
        P("ctx", "head"),
    )
    return jax.shard_map(
        local,
        mesh=mesh,
        in_specs=placed,
        out_specs=(P("ctx", "head"), P("ctx", "head"), P("ctx", "head"), P("ctx", "head")),
        check_vma=False,
    )
```

```python
import functools
import math

import jax
import jax.numpy as jnp
from jax import lax
from jax.experimental import pallas as pl
from jax.experimental.pallas import tpu as pltpu
from jax.sharding import PartitionSpec as P

HD = 128
BLOCK = 512
HALF = BLOCK // 2
WIDTH = 1024
GROUP = 4
KV = 2
ROW = 4
MESH = pl.DeviceIdType.MESH
SCALE = 1.0 / math.sqrt(HD)
EXP2_SCALE = SCALE * math.log2(math.e)
BF16 = jnp.bfloat16
F32 = jnp.float32
OG_CUTS = 2
OG_ROWS = BLOCK // OG_CUTS
CUTS = 2
CUT = WIDTH // CUTS
MOVES = [(n, i * 128, 128) for n in (0, 1) for i in range(4)] + [(n, i * 256, 256) for n in (2, 3) for i in range(2)]


def nn(a, b):
    return lax.dot_general(a, b, (((1,), (0,)), ((), ())), preferred_element_type=F32)


def nt(a, b):
    return lax.dot_general(a, b, (((1,), (1,)), ((), ())), preferred_element_type=F32)


def kernel(
    sel, q_hbm, k_hbm, v_hbm, w_hbm, og_hbm,
    proj_hbm, dq_hbm, dk_hbm, dv_hbm,
    own, win0, win1, vt, kt, qv, wv, ogb, dot_, ot, ob, rl, eb, sb, acc,
    gs0, gs1, gr0, gr1, gxs, gxr, pcs, pcr, pxs, pxr, pown, dqv, dkv_out, dob, rdb, top0, total0, fades,
    lsem, osem, xs, xr, ds_, dr, ocs, ocr, oxs, oxr, ofs, ofr, pcss, pcrs, pxss, pxrs, bds, bdr, bxs, bxr,
):
    win = (win0, win1)
    gs = (gs0, gs1)
    gr = (gr0, gr1)
    ctx = lax.axis_index("ctx")
    head = lax.axis_index("head")
    y = lax.rem(ctx, ROW)
    row_start = ctx - y
    following = lax.rem(ctx + ROW, 32)
    preceding = lax.rem(ctx + 32 - ROW, 32)
    chip = head // 2
    core = lax.rem(head, 2)
    other_core = chip * 2 + 1 - core
    other_chip = (1 - chip) * 2 + core
    diagonal = (1 - chip) * 2 + 1 - core

    def peer(k):
        return row_start + lax.rem(y + k, ROW)

    def remote(src, dst, ss, rs, c, h):
        return pltpu.make_async_remote_copy(
            src_ref=src, dst_ref=dst, send_sem=ss, recv_sem=rs, device_id=(c, h), device_id_type=MESH
        )

    kv_in = []
    for g in range(KV):
        cols = pl.ds(g * HD, HD)
        kv_in.append(
            (
                pltpu.make_async_copy(k_hbm.at[:, cols], own.at[g, 0], lsem.at[2 * g]),
                pltpu.make_async_copy(v_hbm.at[:, cols], own.at[g, 1], lsem.at[2 * g + 1]),
            )
        )
        kv_in[g][0].start()
        kv_in[g][1].start()
    og_in = pltpu.make_async_copy(og_hbm, ogb.at[head], lsem.at[4])
    og_in.start()
    w_in = pltpu.make_async_copy(w_hbm, wv, lsem.at[5])
    w_in.start()
    q_in = pltpu.make_async_copy(q_hbm, qv, lsem.at[6])
    q_in.start()

    barrier = pltpu.get_barrier_semaphore()
    for c, h in (
        (following, head), (preceding, head), (peer(1), head), (peer(2), head), (peer(3), head),
        (ctx, other_core), (ctx, other_chip),
    ):
        pl.semaphore_signal(barrier, inc=1, device_id=(c, h), device_id_type=MESH)
    pl.semaphore_wait(barrier, 7)

    cross = [
        remote(own.at[g], win[g].at[y], xs.at[g], xr.at[g], following, head) for g in range(KV)
    ]
    serve_own = [
        [remote(own.at[g], win[g].at[y], ds_.at[g, k - 1], dr.at[g, k - 1], peer(k), head) for k in (1, 2, 3)]
        for g in range(KV)
    ]
    serve_prev = [
        [remote(win[g].at[y], win[g].at[y], ds_.at[g, k - 1], dr.at[g, k - 1], peer(k), head) for k in (1, 2, 3)]
        for g in range(KV)
    ]
    for g in range(KV):
        kv_in[g][0].wait()
        kv_in[g][1].wait()
        cross[g].start()
        if g == 0:
            for k in (1, 3, 2):
                pl.when(y + k < ROW)(serve_own[g][k - 1].start)

    og_in.wait()
    og_core = remote(ogb.at[head], ogb.at[head], ocs.at[0], ocr.at[0], ctx, other_core)
    og_core.start()
    og_chip = []
    og_pass = []
    for i in range(OG_CUTS):
        rows = pl.ds(i * OG_ROWS, OG_ROWS)
        og_chip.append(
            remote(ogb.at[head, rows], ogb.at[head, rows], oxs.at[i], oxr.at[i], ctx, other_chip)
        )
        og_pass.append(
            remote(ogb.at[other_chip, rows], ogb.at[other_chip, rows], ofs.at[i], ofr.at[i], ctx, other_core)
        )

    def grad_block(block, first):
        cols = pl.ds(pl.multiple_of(block * WIDTH, WIDTH), WIDTH)

        def step(i, _):
            rows = pl.ds(pl.multiple_of(i * 256, 256), 256)
            part = nt(wv[rows, cols], ogb[block])
            dot_[rows, :] = part if first else dot_[rows, :] + part
            return 0

        lax.fori_loop(0, WIDTH // 256, step, 0)

    w_in.wait()
    grad_block(head, True)

    for g in range(KV):
        cross[g].wait_recv()
        for k in (3, 1, 2):
            pl.when(y + k >= ROW)(serve_prev[g][k - 1].start)
        if g == 0:
            for k in (1, 3, 2):
                pl.when(y + k < ROW)(serve_own[1][k - 1].start)
        else:
            for i in range(OG_CUTS):
                og_chip[i].start()
    og_core.wait_recv()
    grad_block(other_core, False)

    sel1 = sel[0, 1]
    sel2 = sel[0, 2]
    col1 = lax.rem(sel1, ROW)
    col2 = lax.rem(sel2, ROW)
    live1 = sel1 != ctx
    live2 = sel2 != ctx

    key_pos = lax.broadcasted_iota(jnp.int32, (HALF, BLOCK), 0)
    query_pos = lax.broadcasted_iota(jnp.int32, (HALF, BLOCK), 1)

    def forward_near(g):
        vt[0] = own[g, 1].T

        def one_head(r, _):
            hh = g * GROUP + r
            hcols = pl.ds(pl.multiple_of(hh * HD, HD), HD)
            q = qv[:, hcols]
            s = nt(own[g, 0, :HALF], q)
            s = jnp.where(key_pos <= query_pos, s, -1e30)
            late = nt(own[g, 0, HALF:], q[HALF:])
            late = jnp.where((key_pos <= query_pos)[:, :HALF], late, -1e30)
            top = jnp.max(s, axis=0, keepdims=True)
            top = jnp.concatenate(
                [top[:, :HALF], jnp.maximum(top[:, HALF:], jnp.max(late, axis=0, keepdims=True))], axis=1
            )
            shift = top * EXP2_SCALE
            e = jnp.exp2(s * EXP2_SCALE - shift)
            e2 = jnp.exp2(late * EXP2_SCALE - shift[:, HALF:])
            total = jnp.sum(e, axis=0, keepdims=True)
            total = jnp.concatenate(
                [total[:, :HALF], total[:, HALF:] + jnp.sum(e2, axis=0, keepdims=True)], axis=1
            )
            e = e.astype(BF16)
            e2 = e2.astype(BF16)
            eb[hh, 0:HALF, :] = e
            eb[hh, HALF:BLOCK, HALF:] = e2
            out = nn(vt[0, :, :HALF], e)
            out2 = nn(vt[0, :, HALF:], e2)
            ot[hcols, :] = jnp.concatenate([out[:, :HALF], out[:, HALF:] + out2], axis=1)
            top0[hh] = top
            total0[hh] = total
            return 0

        lax.fori_loop(0, GROUP, one_head, 0)

    def forward_far(g):
        w_ = win[g]
        vt[1] = w_[col1, 1].T
        vt[2] = w_[col2, 1].T

        def one_head(r, _):
            hh = g * GROUP + r
            hcols = pl.ds(pl.multiple_of(hh * HD, HD), HD)
            q = qv[:, hcols]
            first_top = top0[hh]
            top = first_top
            for j, (col, live) in enumerate(((col1, live1), (col2, live2))):
                for half in range(2):
                    s = nt(w_[col, 0, half * HALF : (half + 1) * HALF], q)
                    sb[BLOCK * j + half * HALF : BLOCK * j + (half + 1) * HALF, :] = s
                    top = jnp.maximum(top, jnp.where(live, jnp.max(s, axis=0, keepdims=True), -1e30))
            shift = top * EXP2_SCALE
            fade = jnp.exp2(first_top * EXP2_SCALE - shift)
            total = total0[hh] * fade
            out = ot[hcols, :] * fade
            for j, live in enumerate((live1, live2)):
                sh = jnp.where(live, shift, 1e30)
                for half in range(2):
                    at = BLOCK * j + half * HALF
                    e = jnp.exp2(sb[at : at + HALF, :] * EXP2_SCALE - sh)
                    total = total + jnp.sum(e, axis=0, keepdims=True)
                    e = e.astype(BF16)
                    eb[hh, BLOCK + at : BLOCK + at + HALF, :] = e
                    out = out + nn(vt[j + 1, :, half * HALF : (half + 1) * HALF], e)
            recip = 1.0 / total
            rl[hh] = recip
            fades[hh] = fade
            out = out * recip
            ot[hcols, :] = out
            ob[:, hcols] = out.T.astype(BF16)
            return 0

        lax.fori_loop(0, GROUP, one_head, 0)

    q_in.wait()
    for g in range(KV):
        forward_near(g)
    for g in range(KV):
        for k in (1, 2, 3):
            serve_own[g][k - 1].wait_recv()
        forward_far(g)

    def project(block, cut, put):
        def step(i, _):
            n0 = pl.multiple_of(i * 256, 256)
            cols = pl.ds(pl.multiple_of(block * WIDTH + cut * CUT + n0, 256), 256)
            put(pl.ds(n0, 256), nn(ob[...], wv[:, cols]))
            return 0

        lax.fori_loop(0, CUT // 256, step, 0)

    def to_core(slot, cut):
        def put(cols, val):
            pcs[slot, cut, :, cols] = val.astype(BF16)

        return put

    def to_chip(cut):
        def put(cols, val):
            pxs[cut, :, cols] = (val + pcr[0, cut, :, cols].astype(F32)).astype(BF16)

        return put

    def keep(cut):
        def put(cols, val):
            pown[cut, :, cols] = val

        return put

    p_core = [
        [remote(pcs.at[i, j], pcr.at[i, j], pcss.at[i, j], pcrs.at[i, j], ctx, other_core) for j in range(CUTS)]
        for i in range(2)
    ]
    p_chip = [remote(pxs.at[j], pxr.at[j], pxss.at[j], pxrs.at[j], ctx, other_chip) for j in range(CUTS)]
    project(diagonal, 0, to_core(0, 0))
    p_core[0][0].start()
    project(diagonal, 1, to_core(0, 1))
    p_core[0][1].start()
    for j in range(CUTS):
        p_core[0][j].wait_recv()
        project(other_chip, j, to_chip(j))
        p_chip[j].start()
        if j == 0:
            for i in range(OG_CUTS):
                og_chip[i].wait_recv()
                og_pass[i].start()
    grad_block(other_chip, False)
    for i in range(OG_CUTS):
        og_pass[i].wait_recv()
    grad_block(diagonal, False)

    def back_tile(g, slot, w_, col, part, hh, q, do, rd, span):
        keys_at = slice(part * HALF, (part + 1) * HALF)
        e = eb[hh, slot * BLOCK + part * HALF : slot * BLOCK + (part + 1) * HALF, span]
        v = own[g, 1, keys_at] if slot == 0 else w_[col, 1, keys_at]
        dp = nn(v, do)
        dsv = (e.astype(F32) * (dp - rd)).astype(BF16)
        acc[g, 0, slot, keys_at] += nn(dsv, q)
        return nn(kt[slot, :, keys_at], dsv)

    def value_far(g):
        for r in range(GROUP):
            hh = g * GROUP + r
            hcols = slice(hh * HD, (hh + 1) * HD)
            do32 = dot_[hcols, :] * rl[hh]
            do = do32.astype(BF16)
            rdb[hh] = jnp.sum(do32 * ot[hcols, :], axis=0, keepdims=True)
            dob[hcols, :] = do
            for slot in (1, 2):
                part = nt(eb[hh, slot * BLOCK : (slot + 1) * BLOCK, :], do)
                acc[g, 1, slot] = part if r == 0 else acc[g, 1, slot] + part

    def backward_far(g):
        w_ = win[g]
        kt[1] = w_[col1, 0].T
        kt[2] = w_[col2, 0].T
        acc[g, 0] = jnp.zeros(acc.shape[2:], F32)

        def one_head(r, _):
            hh = g * GROUP + r
            hcols = pl.ds(pl.multiple_of(hh * HD, HD), HD)
            q = qv[:, hcols]
            do = dob[hcols, :]
            rd = rdb[hh]
            dqt = jnp.zeros((HD, BLOCK), F32)
            for slot, col in ((1, col1), (2, col2)):
                for part in range(2):
                    dqt = dqt + back_tile(g, slot, w_, col, part, hh, q, do, rd, slice(None))
            dot_[hcols, :] = dqt
            return 0

        lax.fori_loop(0, GROUP, one_head, 0, unroll=GROUP)

    def backward_near(g):
        kt[0] = own[g, 0].T
        acc[g, 1, 0] = jnp.zeros((BLOCK, HD), F32)

        def one_head(r, _):
            hh = g * GROUP + r
            hcols = pl.ds(pl.multiple_of(hh * HD, HD), HD)
            q = qv[:, hcols]
            do = (dob[hcols, :].astype(F32) * fades[hh]).astype(BF16)
            rd = rdb[hh] * fades[hh]
            acc[g, 1, 0, :HALF] += nt(eb[hh, :HALF, :], do)
            acc[g, 1, 0, HALF:] += nt(eb[hh, HALF:BLOCK, HALF:], do[:, HALF:])
            dqt = dot_[hcols, :] + back_tile(g, 0, None, None, 0, hh, q, do, rd, slice(None))
            late = back_tile(g, 0, None, None, 1, hh, q[HALF:], do[:, HALF:], rd[:, HALF:], slice(HALF, BLOCK))
            dqt = jnp.concatenate([dqt[:, :HALF], dqt[:, HALF:] + late], axis=1)
            dqv[:, hcols] = (dqt * SCALE).T.astype(BF16)
            return 0

        lax.fori_loop(0, GROUP, one_head, 0, unroll=GROUP)

    give = [
        [
            [
                remote(
                    gs[g].at[lax.rem(y + ROW - k, ROW), part], gr[g].at[k - 1, part],
                    bds.at[g, part, k - 1], bdr.at[g, part, k - 1],
                    row_start + lax.rem(y + ROW - k, ROW), head,
                )
                for k in (1, 2, 3)
            ]
            for part in range(2)
        ]
        for g in range(KV)
    ]
    give_back = [
        [
            remote(gxs.at[g, part], gxr.at[g, part], bxs.at[g, part], bxr.at[g, part], preceding, head)
            for part in range(2)
        ]
        for g in range(KV)
    ]
    factors = (SCALE, 1.0)

    def send_grads(g, part):
        one = acc[g, part, 1] * factors[part]
        two = acc[g, part, 2] * factors[part]
        for c in range(ROW):
            gs[g][c, part] = (jnp.where(col1 == c, one, 0.0) + jnp.where(col2 == c, two, 0.0)).astype(BF16)
        for k in (1, 3, 2):
            give[g][part][k - 1].start()

    def sum_grads(g, part):
        for k in (1, 2, 3):
            give[g][part][k - 1].wait_recv()
        mine = None
        back = gs[g][y, part].astype(F32)
        for k in (1, 2, 3):
            came = gr[g][k - 1, part].astype(F32)
            inside = y + k < ROW
            kept = jnp.where(inside, came, 0.0)
            mine = kept if mine is None else mine + kept
            back = back + jnp.where(inside, 0.0, came)
        gxs[g, part] = back.astype(BF16)
        give_back[g][part].start()
        acc[g, part, 1] = mine

    outs = []

    def finish_grads(g, part):
        give_back[g][part].wait_recv()
        total = acc[g, part, 0] * factors[part] + acc[g, part, 1] + gxr[g, part].astype(F32)
        dkv_out[g, part] = total.astype(BF16)
        ref = (dk_hbm, dv_hbm)[part]
        cp = pltpu.make_async_copy(dkv_out.at[g, part], ref.at[:, pl.ds(g * HD, HD)], osem.at[2 * g + part])
        cp.start()
        outs.append(cp)

    for g in range(KV):
        value_far(g)
        send_grads(g, 1)
    for g in range(KV):
        backward_far(g)
        send_grads(g, 0)
    sum_grads(0, 1)
    backward_near(0)
    sum_grads(1, 1)
    backward_near(1)
    cp = pltpu.make_async_copy(dqv, dq_hbm, osem.at[4])
    cp.start()
    outs.append(cp)
    sum_grads(0, 0)
    for j in range(CUTS):
        project(other_core, j, to_core(1, j))
        p_core[1][j].start()
    for j in range(CUTS):
        project(head, j, keep(j))
    for j in range(CUTS):
        p_core[1][j].wait_recv()
        p_chip[j].wait()
        pxs[j] = (pown[j] + pcr[1, j].astype(F32) + pxr[j].astype(F32)).astype(BF16)
        cp = pltpu.make_async_copy(pxs.at[j], proj_hbm.at[:, pl.ds(j * CUT, CUT)], osem.at[5 + j])
        cp.start()
        outs.append(cp)
    sum_grads(1, 0)
    for g, part in ((0, 1), (1, 1), (0, 0), (1, 0)):
        finish_grads(g, part)

    og_core.wait_send()
    for i in range(OG_CUTS):
        og_chip[i].wait_send()
        og_pass[i].wait_send()
    for i in range(2):
        for j in range(CUTS):
            p_core[i][j].wait_send()
    for g in range(KV):
        cross[g].wait_send()
        for k in (1, 2, 3):
            serve_own[g][k - 1].wait_send()
        for part in range(2):
            give_back[g][part].wait_send()
            for k in (1, 2, 3):
                give[g][part][k - 1].wait_send()
    for cp in outs:
        cp.wait()


def mover(*refs):
    ins, outs, held, sems = refs[:4], refs[4:8], refs[8:12], refs[12]
    copies = []
    for i, (n, first, rows) in enumerate(MOVES):
        at = pl.ds(first, rows)
        copies.append(
            (
                pltpu.make_async_copy(ins[n].at[at], held[n].at[at], sems.at[0, i]),
                pltpu.make_async_copy(held[n].at[at], outs[n].at[at], sems.at[1, i]),
            )
        )
    for come, _ in copies:
        come.start()
    for come, go in copies:
        come.wait()
        go.start()
    for _, go in copies:
        go.wait()


def local(queries, keys, values, selected, out_weight, out_grad):
    vm = pltpu.VMEM
    dma = pltpu.SemaphoreType.DMA
    anyspec = pl.BlockSpec(memory_space=pl.ANY)
    shapes = (
        jax.ShapeDtypeStruct((BLOCK, WIDTH), BF16),
        jax.ShapeDtypeStruct((BLOCK, WIDTH), BF16),
        jax.ShapeDtypeStruct((BLOCK, KV * HD), BF16),
        jax.ShapeDtypeStruct((BLOCK, KV * HD), BF16),
    )
    results = pl.pallas_call(
        kernel,
        out_shape=shapes,
        in_specs=[pl.BlockSpec(memory_space=pltpu.SMEM)] + [anyspec] * 5,
        out_specs=(anyspec,) * 4,
        scratch_shapes=[
            vm((KV, 2, BLOCK, HD), BF16),
            vm((ROW, 2, BLOCK, HD), BF16),
            vm((ROW, 2, BLOCK, HD), BF16),
            vm((3, HD, BLOCK), BF16),
            vm((3, HD, BLOCK), BF16),
            vm((BLOCK, WIDTH), BF16),
            vm((WIDTH, 4 * WIDTH), BF16),
            vm((4, BLOCK, WIDTH), BF16),
            vm((WIDTH, BLOCK), F32),
            vm((WIDTH, BLOCK), F32),
            vm((BLOCK, WIDTH), BF16),
            vm((KV * GROUP, 1, BLOCK), F32),
            vm((KV * GROUP, 3 * BLOCK, BLOCK), BF16),
            vm((2 * BLOCK, BLOCK), F32),
            vm((KV, 2, 3, BLOCK, HD), F32),
            vm((ROW, 2, BLOCK, HD), BF16),
            vm((ROW, 2, BLOCK, HD), BF16),
            vm((3, 2, BLOCK, HD), BF16),
            vm((3, 2, BLOCK, HD), BF16),
            vm((KV, 2, BLOCK, HD), BF16),
            vm((KV, 2, BLOCK, HD), BF16),
            vm((2, CUTS, BLOCK, CUT), BF16),
            vm((2, CUTS, BLOCK, CUT), BF16),
            vm((CUTS, BLOCK, CUT), BF16),
            vm((CUTS, BLOCK, CUT), BF16),
            vm((CUTS, BLOCK, CUT), F32),
            vm((BLOCK, WIDTH), BF16),
            vm((KV, 2, BLOCK, HD), BF16),
            vm((WIDTH, BLOCK), BF16),
            vm((KV * GROUP, 1, BLOCK), F32),
            vm((KV * GROUP, 1, BLOCK), F32),
            vm((KV * GROUP, 1, BLOCK), F32),
            vm((KV * GROUP, 1, BLOCK), F32),
            dma((7,)), dma((5 + CUTS,)),
            dma((KV,)), dma((KV,)), dma((KV, 3)), dma((KV, 3)),
            dma((1,)), dma((1,)), dma((OG_CUTS,)), dma((OG_CUTS,)), dma((OG_CUTS,)), dma((OG_CUTS,)),
            dma((2, CUTS)), dma((2, CUTS)), dma((CUTS,)), dma((CUTS,)),
            dma((KV, 2, 3)), dma((KV, 2, 3)), dma((KV, 2)), dma((KV, 2)),
        ],
        compiler_params=pltpu.CompilerParams(
            collective_id=0, has_side_effects=True, vmem_limit_bytes=63 * 1024 * 1024
        ),
        cost_estimate=pl.CostEstimate(flops=18 * 10**9, bytes_accessed=16 * 2**20, transcendentals=6 * 10**6),
        name="layer",
    )(selected, queries, keys, values, out_weight, out_grad)
    return pl.pallas_call(
        mover,
        out_shape=shapes,
        in_specs=[anyspec] * 4,
        out_specs=(anyspec,) * 4,
        scratch_shapes=[vm(x.shape, x.dtype) for x in shapes] + [dma((2, len(MOVES)))],
        compiler_params=pltpu.CompilerParams(vmem_limit_bytes=60 * 1024 * 1024),
        name="move",
    )(*results)


def solution(mesh):
    placed = (
        P("ctx", "head"),
        P("ctx", "head"),
        P("ctx", "head"),
        P("ctx", None),
        P("head", None),
        P("ctx", "head"),
    )
    return jax.shard_map(
        local,
        mesh=mesh,
        in_specs=placed,
        out_specs=(P("ctx", "head"), P("ctx", "head"), P("ctx", "head"), P("ctx", "head")),
        check_vma=False,
    )
```

```python
import functools
import math

import jax
import jax.numpy as jnp
from jax import lax
from jax.experimental import pallas as pl
from jax.experimental.pallas import tpu as pltpu
from jax.sharding import PartitionSpec as P

HD = 128
BLOCK = 512
HALF = BLOCK // 2
WIDTH = 1024
GROUP = 4
KV = 2
ROW = 4
MESH = pl.DeviceIdType.MESH
SCALE = 1.0 / math.sqrt(HD)
EXP2_SCALE = SCALE * math.log2(math.e)
BF16 = jnp.bfloat16
F32 = jnp.float32
OG_CUTS = 2
OG_ROWS = BLOCK // OG_CUTS
CUTS = 2
CUT = WIDTH // CUTS
MOVES = [(n, i * 128, 128) for n in (0, 1) for i in range(4)] + [(n, i * 256, 256) for n in (2, 3) for i in range(2)]


def nn(a, b):
    return lax.dot_general(a, b, (((1,), (0,)), ((), ())), preferred_element_type=F32)


def nt(a, b):
    return lax.dot_general(a, b, (((1,), (1,)), ((), ())), preferred_element_type=F32)


def kernel(
    sel, q_hbm, k_hbm, v_hbm, w_hbm, og_hbm,
    proj_hbm, dq_hbm, dk_hbm, dv_hbm,
    own, wink0, winv0, wink1, winv1, vt, kt, qv, wv, ogb, dot_, ot, ob, rl, eb, sb, acc,
    gs0, gs1, gr0, gr1, gxs, gxr, pcs, pcr, pxs, pxr, pown, dqv, dkv_out, dob, rdb, top0, total0, fades,
    lsem, osem, xs, xr, ds_, dr, ocs, ocr, oxs, oxr, ofs, ofr, pcss, pcrs, pxss, pxrs, bds, bdr, bxs, bxr,
):
    win = ((wink0, winv0), (wink1, winv1))
    gs = (gs0, gs1)
    gr = (gr0, gr1)
    ctx = lax.axis_index("ctx")
    head = lax.axis_index("head")
    y = lax.rem(ctx, ROW)
    row_start = ctx - y
    following = lax.rem(ctx + ROW, 32)
    preceding = lax.rem(ctx + 32 - ROW, 32)
    chip = head // 2
    core = lax.rem(head, 2)
    other_core = chip * 2 + 1 - core
    other_chip = (1 - chip) * 2 + core
    diagonal = (1 - chip) * 2 + 1 - core

    def peer(k):
        return row_start + lax.rem(y + k, ROW)

    def remote(src, dst, ss, rs, c, h):
        return pltpu.make_async_remote_copy(
            src_ref=src, dst_ref=dst, send_sem=ss, recv_sem=rs, device_id=(c, h), device_id_type=MESH
        )

    kv_in = []
    for g in range(KV):
        cols = pl.ds(g * HD, HD)
        kv_in.append(
            (
                pltpu.make_async_copy(k_hbm.at[:, cols], own.at[g, 0], lsem.at[2 * g]),
                pltpu.make_async_copy(v_hbm.at[:, cols], own.at[g, 1], lsem.at[2 * g + 1]),
            )
        )
        kv_in[g][0].start()
        kv_in[g][1].start()
    og_in = pltpu.make_async_copy(og_hbm, ogb.at[head], lsem.at[4])
    og_in.start()
    w_in = pltpu.make_async_copy(w_hbm, wv, lsem.at[5])
    w_in.start()
    q_in = pltpu.make_async_copy(q_hbm, qv, lsem.at[6])
    q_in.start()

    barrier = pltpu.get_barrier_semaphore()
    for c, h in (
        (following, head), (preceding, head), (peer(1), head), (peer(2), head), (peer(3), head),
        (ctx, other_core), (ctx, other_chip),
    ):
        pl.semaphore_signal(barrier, inc=1, device_id=(c, h), device_id_type=MESH)
    pl.semaphore_wait(barrier, 7)

    pieces = [(g, part) for part in range(2) for g in range(KV)]
    cross = {
        (g, p): remote(own.at[g, p], win[g][p].at[y], xs.at[g, p], xr.at[g, p], following, head) for g, p in pieces
    }
    serve_own = {
        (g, p, k): remote(own.at[g, p], win[g][p].at[y], ds_.at[g, p, k - 1], dr.at[g, p, k - 1], peer(k), head)
        for g, p in pieces
        for k in (1, 2, 3)
    }
    serve_prev = {
        (g, p, k): remote(win[g][p].at[y], win[g][p].at[y], ds_.at[g, p, k - 1], dr.at[g, p, k - 1], peer(k), head)
        for g, p in pieces
        for k in (1, 2, 3)
    }

    def start_own(g, p):
        for k in (1, 3, 2):
            pl.when(y + k < ROW)(serve_own[g, p, k].start)

    def pass_on(g, p):
        cross[g, p].wait_recv()
        for k in (3, 1, 2):
            pl.when(y + k >= ROW)(serve_prev[g, p, k].start)

    def arrived(g, p):
        for k in (1, 2, 3):
            serve_own[g, p, k].wait_recv()

    for g, p in pieces:
        kv_in[g][p].wait()
        cross[g, p].start()
        if p == 0:
            start_own(g, p)

    og_in.wait()
    og_core = remote(ogb.at[head], ogb.at[head], ocs.at[0], ocr.at[0], ctx, other_core)
    og_core.start()
    og_chip = []
    og_pass = []
    for i in range(OG_CUTS):
        rows = pl.ds(i * OG_ROWS, OG_ROWS)
        og_chip.append(
            remote(ogb.at[head, rows], ogb.at[head, rows], oxs.at[i], oxr.at[i], ctx, other_chip)
        )
        og_pass.append(
            remote(ogb.at[other_chip, rows], ogb.at[other_chip, rows], ofs.at[i], ofr.at[i], ctx, other_core)
        )

    def grad_block(block, first):
        cols = pl.ds(pl.multiple_of(block * WIDTH, WIDTH), WIDTH)

        def step(i, _):
            rows = pl.ds(pl.multiple_of(i * 256, 256), 256)
            part = nt(wv[rows, cols], ogb[block])
            dot_[rows, :] = part if first else dot_[rows, :] + part
            return 0

        lax.fori_loop(0, WIDTH // 256, step, 0)

    w_in.wait()
    grad_block(head, True)

    pass_on(0, 0)
    pass_on(1, 0)
    start_own(0, 1)
    pass_on(0, 1)
    start_own(1, 1)
    pass_on(1, 1)
    for i in range(OG_CUTS):
        og_chip[i].start()
    og_core.wait_recv()
    grad_block(other_core, False)

    sel1 = sel[0, 1]
    sel2 = sel[0, 2]
    col1 = lax.rem(sel1, ROW)
    col2 = lax.rem(sel2, ROW)
    live1 = sel1 != ctx
    live2 = sel2 != ctx

    key_pos = lax.broadcasted_iota(jnp.int32, (HALF, BLOCK), 0)
    query_pos = lax.broadcasted_iota(jnp.int32, (HALF, BLOCK), 1)

    def forward_near(g):
        vt[0] = own[g, 1].T

        def one_head(r, _):
            hh = g * GROUP + r
            hcols = pl.ds(pl.multiple_of(hh * HD, HD), HD)
            q = qv[:, hcols]
            s = nt(own[g, 0, :HALF], q)
            s = jnp.where(key_pos <= query_pos, s, -1e30)
            late = nt(own[g, 0, HALF:], q[HALF:])
            late = jnp.where((key_pos <= query_pos)[:, :HALF], late, -1e30)
            top = jnp.max(s, axis=0, keepdims=True)
            top = jnp.concatenate(
                [top[:, :HALF], jnp.maximum(top[:, HALF:], jnp.max(late, axis=0, keepdims=True))], axis=1
            )
            shift = top * EXP2_SCALE
            e = jnp.exp2(s * EXP2_SCALE - shift)
            e2 = jnp.exp2(late * EXP2_SCALE - shift[:, HALF:])
            total = jnp.sum(e, axis=0, keepdims=True)
            total = jnp.concatenate(
                [total[:, :HALF], total[:, HALF:] + jnp.sum(e2, axis=0, keepdims=True)], axis=1
            )
            e = e.astype(BF16)
            e2 = e2.astype(BF16)
            eb[hh, 0:HALF, :] = e
            eb[hh, HALF:BLOCK, HALF:] = e2
            out = nn(vt[0, :, :HALF], e)
            out2 = nn(vt[0, :, HALF:], e2)
            ot[hcols, :] = jnp.concatenate([out[:, :HALF], out[:, HALF:] + out2], axis=1)
            top0[hh] = top
            total0[hh] = total
            return 0

        lax.fori_loop(0, GROUP, one_head, 0)

    def scores_far(g):
        w_ = win[g]

        def one_head(r, _):
            hh = g * GROUP + r
            hcols = pl.ds(pl.multiple_of(hh * HD, HD), HD)
            q = qv[:, hcols]
            first_top = top0[hh]
            top = first_top
            for j, (col, live) in enumerate(((col1, live1), (col2, live2))):
                for half in range(2):
                    s = nt(w_[0][col, half * HALF : (half + 1) * HALF], q)
                    sb[BLOCK * j + half * HALF : BLOCK * j + (half + 1) * HALF, :] = s
                    top = jnp.maximum(top, jnp.where(live, jnp.max(s, axis=0, keepdims=True), -1e30))
            shift = top * EXP2_SCALE
            fade = jnp.exp2(first_top * EXP2_SCALE - shift)
            total = total0[hh] * fade
            for j, live in enumerate((live1, live2)):
                sh = jnp.where(live, shift, 1e30)
                for half in range(2):
                    at = BLOCK * j + half * HALF
                    e = jnp.exp2(sb[at : at + HALF, :] * EXP2_SCALE - sh)
                    total = total + jnp.sum(e, axis=0, keepdims=True)
                    eb[hh, BLOCK + at : BLOCK + at + HALF, :] = e.astype(BF16)
            rl[hh] = 1.0 / total
            fades[hh] = fade
            return 0

        lax.fori_loop(0, GROUP, one_head, 0)

    def values_far(g):
        w_ = win[g]
        vt[1] = w_[1][col1].T
        vt[2] = w_[1][col2].T

        def one_head(r, _):
            hh = g * GROUP + r
            hcols = pl.ds(pl.multiple_of(hh * HD, HD), HD)
            out = ot[hcols, :] * fades[hh]
            out = out + nn(vt[1], eb[hh, BLOCK : 2 * BLOCK, :]) + nn(vt[2], eb[hh, 2 * BLOCK :, :])
            out = out * rl[hh]
            ot[hcols, :] = out
            ob[:, hcols] = out.T.astype(BF16)
            return 0

        lax.fori_loop(0, GROUP, one_head, 0, unroll=2)

    q_in.wait()
    for g in range(KV):
        forward_near(g)
    for g in range(KV):
        arrived(g, 0)
        scores_far(g)
    for g in range(KV):
        arrived(g, 1)
        values_far(g)

    def project(block, cut, put):
        def step(i, _):
            n0 = pl.multiple_of(i * 256, 256)
            cols = pl.ds(pl.multiple_of(block * WIDTH + cut * CUT + n0, 256), 256)
            put(pl.ds(n0, 256), nn(ob[...], wv[:, cols]))
            return 0

        lax.fori_loop(0, CUT // 256, step, 0)

    def to_core(slot, cut):
        def put(cols, val):
            pcs[slot, cut, :, cols] = val.astype(BF16)

        return put

    def to_chip(cut):
        def put(cols, val):
            pxs[cut, :, cols] = (val + pcr[0, cut, :, cols].astype(F32)).astype(BF16)

        return put

    def keep(cut):
        def put(cols, val):
            pown[cut, :, cols] = val

        return put

    p_core = [
        [remote(pcs.at[i, j], pcr.at[i, j], pcss.at[i, j], pcrs.at[i, j], ctx, other_core) for j in range(CUTS)]
        for i in range(2)
    ]
    p_chip = [remote(pxs.at[j], pxr.at[j], pxss.at[j], pxrs.at[j], ctx, other_chip) for j in range(CUTS)]
    project(diagonal, 0, to_core(0, 0))
    p_core[0][0].start()
    project(diagonal, 1, to_core(0, 1))
    p_core[0][1].start()
    for j in range(CUTS):
        p_core[0][j].wait_recv()
        project(other_chip, j, to_chip(j))
        p_chip[j].start()
        if j == 0:
            for i in range(OG_CUTS):
                og_chip[i].wait_recv()
                og_pass[i].start()
    grad_block(other_chip, False)
    for i in range(OG_CUTS):
        og_pass[i].wait_recv()
    grad_block(diagonal, False)

    def back_tile(g, slot, w_, col, part, hh, q, do, rd, span):
        keys_at = slice(part * HALF, (part + 1) * HALF)
        e = eb[hh, slot * BLOCK + part * HALF : slot * BLOCK + (part + 1) * HALF, span]
        v = own[g, 1, keys_at] if slot == 0 else w_[1][col, keys_at]
        dp = nn(v, do)
        dsv = (e.astype(F32) * (dp - rd)).astype(BF16)
        acc[g, 0, slot, keys_at] += nn(dsv, q)
        return nn(kt[slot, :, keys_at], dsv)

    def value_far(g):
        for r in range(GROUP):
            hh = g * GROUP + r
            hcols = slice(hh * HD, (hh + 1) * HD)
            do32 = dot_[hcols, :] * rl[hh]
            do = do32.astype(BF16)
            rdb[hh] = jnp.sum(do32 * ot[hcols, :], axis=0, keepdims=True)
            dob[hcols, :] = do
            for slot in (1, 2):
                part = nt(eb[hh, slot * BLOCK : (slot + 1) * BLOCK, :], do)
                acc[g, 1, slot] = part if r == 0 else acc[g, 1, slot] + part

    def backward_far(g):
        w_ = win[g]
        kt[1] = w_[0][col1].T
        kt[2] = w_[0][col2].T
        acc[g, 0] = jnp.zeros(acc.shape[2:], F32)

        def one_head(r, _):
            hh = g * GROUP + r
            hcols = pl.ds(pl.multiple_of(hh * HD, HD), HD)
            q = qv[:, hcols]
            do = dob[hcols, :]
            rd = rdb[hh]
            dqt = jnp.zeros((HD, BLOCK), F32)
            for slot, col in ((1, col1), (2, col2)):
                for part in range(2):
                    dqt = dqt + back_tile(g, slot, w_, col, part, hh, q, do, rd, slice(None))
            dot_[hcols, :] = dqt
            return 0

        lax.fori_loop(0, GROUP, one_head, 0, unroll=GROUP)

    def backward_near(g):
        kt[0] = own[g, 0].T
        acc[g, 1, 0] = jnp.zeros((BLOCK, HD), F32)

        def one_head(r, _):
            hh = g * GROUP + r
            hcols = pl.ds(pl.multiple_of(hh * HD, HD), HD)
            q = qv[:, hcols]
            do = (dob[hcols, :].astype(F32) * fades[hh]).astype(BF16)
            rd = rdb[hh] * fades[hh]
            acc[g, 1, 0, :HALF] += nt(eb[hh, :HALF, :], do)
            acc[g, 1, 0, HALF:] += nt(eb[hh, HALF:BLOCK, HALF:], do[:, HALF:])
            dqt = dot_[hcols, :] + back_tile(g, 0, None, None, 0, hh, q, do, rd, slice(None))
            late = back_tile(g, 0, None, None, 1, hh, q[HALF:], do[:, HALF:], rd[:, HALF:], slice(HALF, BLOCK))
            dqt = jnp.concatenate([dqt[:, :HALF], dqt[:, HALF:] + late], axis=1)
            dqv[:, hcols] = (dqt * SCALE).T.astype(BF16)
            return 0

        lax.fori_loop(0, GROUP, one_head, 0, unroll=GROUP)

    give = [
        [
            [
                remote(
                    gs[g].at[lax.rem(y + ROW - k, ROW), part], gr[g].at[k - 1, part],
                    bds.at[g, part, k - 1], bdr.at[g, part, k - 1],
                    row_start + lax.rem(y + ROW - k, ROW), head,
                )
                for k in (1, 2, 3)
            ]
            for part in range(2)
        ]
        for g in range(KV)
    ]
    give_back = [
        [
            remote(gxs.at[g, part], gxr.at[g, part], bxs.at[g, part], bxr.at[g, part], preceding, head)
            for part in range(2)
        ]
        for g in range(KV)
    ]
    factors = (SCALE, 1.0)

    def send_grads(g, part):
        one = acc[g, part, 1] * factors[part]
        two = acc[g, part, 2] * factors[part]
        for c in range(ROW):
            gs[g][c, part] = (jnp.where(col1 == c, one, 0.0) + jnp.where(col2 == c, two, 0.0)).astype(BF16)
        for k in (1, 3, 2):
            give[g][part][k - 1].start()

    def sum_grads(g, part):
        for k in (1, 2, 3):
            give[g][part][k - 1].wait_recv()
        mine = None
        back = gs[g][y, part].astype(F32)
        for k in (1, 2, 3):
            came = gr[g][k - 1, part].astype(F32)
            inside = y + k < ROW
            kept = jnp.where(inside, came, 0.0)
            mine = kept if mine is None else mine + kept
            back = back + jnp.where(inside, 0.0, came)
        gxs[g, part] = back.astype(BF16)
        give_back[g][part].start()
        acc[g, part, 1] = mine

    outs = []

    def finish_grads(g, part):
        give_back[g][part].wait_recv()
        total = acc[g, part, 0] * factors[part] + acc[g, part, 1] + gxr[g, part].astype(F32)
        dkv_out[g, part] = total.astype(BF16)
        ref = (dk_hbm, dv_hbm)[part]
        cp = pltpu.make_async_copy(dkv_out.at[g, part], ref.at[:, pl.ds(g * HD, HD)], osem.at[2 * g + part])
        cp.start()
        outs.append(cp)

    for g in range(KV):
        value_far(g)
        send_grads(g, 1)
    for g in range(KV):
        backward_far(g)
        send_grads(g, 0)
    sum_grads(0, 1)
    backward_near(0)
    sum_grads(1, 1)
    backward_near(1)
    cp = pltpu.make_async_copy(dqv, dq_hbm, osem.at[4])
    cp.start()
    outs.append(cp)
    sum_grads(0, 0)
    for j in range(CUTS):
        project(other_core, j, to_core(1, j))
        p_core[1][j].start()
    for j in range(CUTS):
        project(head, j, keep(j))
    for j in range(CUTS):
        p_core[1][j].wait_recv()
        p_chip[j].wait()
        pxs[j] = (pown[j] + pcr[1, j].astype(F32) + pxr[j].astype(F32)).astype(BF16)
        cp = pltpu.make_async_copy(pxs.at[j], proj_hbm.at[:, pl.ds(j * CUT, CUT)], osem.at[5 + j])
        cp.start()
        outs.append(cp)
    sum_grads(1, 0)
    for g, part in ((0, 1), (1, 1), (0, 0), (1, 0)):
        finish_grads(g, part)

    og_core.wait_send()
    for i in range(OG_CUTS):
        og_chip[i].wait_send()
        og_pass[i].wait_send()
    for i in range(2):
        for j in range(CUTS):
            p_core[i][j].wait_send()
    for g in range(KV):
        for part in range(2):
            cross[g, part].wait_send()
            for k in (1, 2, 3):
                serve_own[g, part, k].wait_send()
            give_back[g][part].wait_send()
            for k in (1, 2, 3):
                give[g][part][k - 1].wait_send()
    for cp in outs:
        cp.wait()


def mover(*refs):
    ins, outs, held, sems = refs[:4], refs[4:8], refs[8:12], refs[12]
    copies = []
    for i, (n, first, rows) in enumerate(MOVES):
        at = pl.ds(first, rows)
        copies.append(
            (
                pltpu.make_async_copy(ins[n].at[at], held[n].at[at], sems.at[0, i]),
                pltpu.make_async_copy(held[n].at[at], outs[n].at[at], sems.at[1, i]),
            )
        )
    for come, _ in copies:
        come.start()
    for come, go in copies:
        come.wait()
        go.start()
    for _, go in copies:
        go.wait()


def local(queries, keys, values, selected, out_weight, out_grad):
    vm = pltpu.VMEM
    dma = pltpu.SemaphoreType.DMA
    anyspec = pl.BlockSpec(memory_space=pl.ANY)
    shapes = (
        jax.ShapeDtypeStruct((BLOCK, WIDTH), BF16),
        jax.ShapeDtypeStruct((BLOCK, WIDTH), BF16),
        jax.ShapeDtypeStruct((BLOCK, KV * HD), BF16),
        jax.ShapeDtypeStruct((BLOCK, KV * HD), BF16),
    )
    results = pl.pallas_call(
        kernel,
        out_shape=shapes,
        in_specs=[pl.BlockSpec(memory_space=pltpu.SMEM)] + [anyspec] * 5,
        out_specs=(anyspec,) * 4,
        scratch_shapes=[
            vm((KV, 2, BLOCK, HD), BF16),
            vm((ROW, BLOCK, HD), BF16),
            vm((ROW, BLOCK, HD), BF16),
            vm((ROW, BLOCK, HD), BF16),
            vm((ROW, BLOCK, HD), BF16),
            vm((3, HD, BLOCK), BF16),
            vm((3, HD, BLOCK), BF16),
            vm((BLOCK, WIDTH), BF16),
            vm((WIDTH, 4 * WIDTH), BF16),
            vm((4, BLOCK, WIDTH), BF16),
            vm((WIDTH, BLOCK), F32),
            vm((WIDTH, BLOCK), F32),
            vm((BLOCK, WIDTH), BF16),
            vm((KV * GROUP, 1, BLOCK), F32),
            vm((KV * GROUP, 3 * BLOCK, BLOCK), BF16),
            vm((2 * BLOCK, BLOCK), F32),
            vm((KV, 2, 3, BLOCK, HD), F32),
            vm((ROW, 2, BLOCK, HD), BF16),
            vm((ROW, 2, BLOCK, HD), BF16),
            vm((3, 2, BLOCK, HD), BF16),
            vm((3, 2, BLOCK, HD), BF16),
            vm((KV, 2, BLOCK, HD), BF16),
            vm((KV, 2, BLOCK, HD), BF16),
            vm((2, CUTS, BLOCK, CUT), BF16),
            vm((2, CUTS, BLOCK, CUT), BF16),
            vm((CUTS, BLOCK, CUT), BF16),
            vm((CUTS, BLOCK, CUT), BF16),
            vm((CUTS, BLOCK, CUT), F32),
            vm((BLOCK, WIDTH), BF16),
            vm((KV, 2, BLOCK, HD), BF16),
            vm((WIDTH, BLOCK), BF16),
            vm((KV * GROUP, 1, BLOCK), F32),
            vm((KV * GROUP, 1, BLOCK), F32),
            vm((KV * GROUP, 1, BLOCK), F32),
            vm((KV * GROUP, 1, BLOCK), F32),
            dma((7,)), dma((5 + CUTS,)),
            dma((KV, 2)), dma((KV, 2)), dma((KV, 2, 3)), dma((KV, 2, 3)),
            dma((1,)), dma((1,)), dma((OG_CUTS,)), dma((OG_CUTS,)), dma((OG_CUTS,)), dma((OG_CUTS,)),
            dma((2, CUTS)), dma((2, CUTS)), dma((CUTS,)), dma((CUTS,)),
            dma((KV, 2, 3)), dma((KV, 2, 3)), dma((KV, 2)), dma((KV, 2)),
        ],
        compiler_params=pltpu.CompilerParams(
            collective_id=0, has_side_effects=True, vmem_limit_bytes=63 * 1024 * 1024
        ),
        cost_estimate=pl.CostEstimate(flops=18 * 10**9, bytes_accessed=16 * 2**20, transcendentals=6 * 10**6),
        name="layer",
    )(selected, queries, keys, values, out_weight, out_grad)
    return pl.pallas_call(
        mover,
        out_shape=shapes,
        in_specs=[anyspec] * 4,
        out_specs=(anyspec,) * 4,
        scratch_shapes=[vm(x.shape, x.dtype) for x in shapes] + [dma((2, len(MOVES)))],
        compiler_params=pltpu.CompilerParams(vmem_limit_bytes=60 * 1024 * 1024),
        name="move",
    )(*results)


def solution(mesh):
    placed = (
        P("ctx", "head"),
        P("ctx", "head"),
        P("ctx", "head"),
        P("ctx", None),
        P("head", None),
        P("ctx", "head"),
    )
    return jax.shard_map(
        local,
        mesh=mesh,
        in_specs=placed,
        out_specs=(P("ctx", "head"), P("ctx", "head"), P("ctx", "head"), P("ctx", "head")),
        check_vma=False,
    )
```

```python
import functools
import math

import jax
import jax.numpy as jnp
from jax import lax
from jax.experimental import pallas as pl
from jax.experimental.pallas import tpu as pltpu
from jax.sharding import PartitionSpec as P

HD = 128
BLOCK = 512
HALF = BLOCK // 2
WIDTH = 1024
GROUP = 4
KV = 2
ROW = 4
MESH = pl.DeviceIdType.MESH
SCALE = 1.0 / math.sqrt(HD)
EXP2_SCALE = SCALE * math.log2(math.e)
BF16 = jnp.bfloat16
F32 = jnp.float32
OG_CUTS = 2
OG_ROWS = BLOCK // OG_CUTS
CUTS = 2
CUT = WIDTH // CUTS
MOVES = [(n, i * 128, 128) for n in (0, 1) for i in range(4)] + [(n, i * 256, 256) for n in (2, 3) for i in range(2)]


def nn(a, b):
    return lax.dot_general(a, b, (((1,), (0,)), ((), ())), preferred_element_type=F32)


def nt(a, b):
    return lax.dot_general(a, b, (((1,), (1,)), ((), ())), preferred_element_type=F32)


def kernel(
    sel, q_hbm, k_hbm, v_hbm, w_hbm, og_hbm,
    proj_hbm, dq_hbm, dk_hbm, dv_hbm,
    own, wink0, winv0, wink1, winv1, vt, kt, qv, wv, ogb, dot_, ot, ob, rl, eb, sb, acc,
    gs0, gs1, gr0, gr1, gxs, gxr, pcs, pcr, pxs, pxr, pown, dqv, dkv_out, dob, rdb, top0, total0, fades, pdiag,
    lsem, osem, xs, xr, ds_, dr, ocs, ocr, oxs, oxr, ofs, ofr, pcss, pcrs, pxss, pxrs, bds, bdr, bxs, bxr,
):
    win = ((wink0, winv0), (wink1, winv1))
    gs = (gs0, gs1)
    gr = (gr0, gr1)
    ctx = lax.axis_index("ctx")
    head = lax.axis_index("head")
    y = lax.rem(ctx, ROW)
    row_start = ctx - y
    following = lax.rem(ctx + ROW, 32)
    preceding = lax.rem(ctx + 32 - ROW, 32)
    chip = head // 2
    core = lax.rem(head, 2)
    other_core = chip * 2 + 1 - core
    other_chip = (1 - chip) * 2 + core
    diagonal = (1 - chip) * 2 + 1 - core

    def peer(k):
        return row_start + lax.rem(y + k, ROW)

    def remote(src, dst, ss, rs, c, h):
        return pltpu.make_async_remote_copy(
            src_ref=src, dst_ref=dst, send_sem=ss, recv_sem=rs, device_id=(c, h), device_id_type=MESH
        )

    kv_in = []
    for g in range(KV):
        cols = pl.ds(g * HD, HD)
        kv_in.append(
            (
                pltpu.make_async_copy(k_hbm.at[:, cols], own.at[g, 0], lsem.at[2 * g]),
                pltpu.make_async_copy(v_hbm.at[:, cols], own.at[g, 1], lsem.at[2 * g + 1]),
            )
        )
        kv_in[g][0].start()
        kv_in[g][1].start()
    og_in = pltpu.make_async_copy(og_hbm, ogb.at[head], lsem.at[4])
    og_in.start()
    w_in = pltpu.make_async_copy(w_hbm, wv, lsem.at[5])
    w_in.start()
    q_in = pltpu.make_async_copy(q_hbm, qv, lsem.at[6])
    q_in.start()

    barrier = pltpu.get_barrier_semaphore()
    for c, h in (
        (following, head), (preceding, head), (peer(1), head), (peer(2), head), (peer(3), head),
        (ctx, other_core), (ctx, other_chip),
    ):
        pl.semaphore_signal(barrier, inc=1, device_id=(c, h), device_id_type=MESH)
    pl.semaphore_wait(barrier, 7)

    pieces = [(g, part) for part in range(2) for g in range(KV)]
    cross = {
        (g, p): remote(own.at[g, p], win[g][p].at[y], xs.at[g, p], xr.at[g, p], following, head) for g, p in pieces
    }
    serve_own = {
        (g, p, k): remote(own.at[g, p], win[g][p].at[y], ds_.at[g, p, k - 1], dr.at[g, p, k - 1], peer(k), head)
        for g, p in pieces
        for k in (1, 2, 3)
    }
    serve_prev = {
        (g, p, k): remote(win[g][p].at[y], win[g][p].at[y], ds_.at[g, p, k - 1], dr.at[g, p, k - 1], peer(k), head)
        for g, p in pieces
        for k in (1, 2, 3)
    }

    def start_own(g, p):
        for k in (1, 3, 2):
            pl.when(y + k < ROW)(serve_own[g, p, k].start)

    def pass_on(g, p):
        cross[g, p].wait_recv()
        for k in (3, 1, 2):
            pl.when(y + k >= ROW)(serve_prev[g, p, k].start)

    def arrived(g, p):
        for k in (1, 2, 3):
            serve_own[g, p, k].wait_recv()

    for g, p in pieces:
        kv_in[g][p].wait()
        cross[g, p].start()
        if p == 0:
            start_own(g, p)

    og_in.wait()
    og_core = remote(ogb.at[head], ogb.at[head], ocs.at[0], ocr.at[0], ctx, other_core)
    og_core.start()
    og_chip = []
    og_pass = []
    for i in range(OG_CUTS):
        rows = pl.ds(i * OG_ROWS, OG_ROWS)
        og_chip.append(
            remote(ogb.at[head, rows], ogb.at[head, rows], oxs.at[i], oxr.at[i], ctx, other_chip)
        )
        og_pass.append(
            remote(ogb.at[other_chip, rows], ogb.at[other_chip, rows], ofs.at[i], ofr.at[i], ctx, other_core)
        )

    def grad_block(block, first):
        cols = pl.ds(pl.multiple_of(block * WIDTH, WIDTH), WIDTH)

        def step(i, _):
            rows = pl.ds(pl.multiple_of(i * 256, 256), 256)
            part = nt(wv[rows, cols], ogb[block])
            dot_[rows, :] = part if first else dot_[rows, :] + part
            return 0

        lax.fori_loop(0, WIDTH // 256, step, 0)

    w_in.wait()
    grad_block(head, True)

    pass_on(0, 0)
    pass_on(1, 0)
    start_own(0, 1)
    pass_on(0, 1)
    start_own(1, 1)
    pass_on(1, 1)
    for i in range(OG_CUTS):
        og_chip[i].start()
    og_core.wait_recv()
    grad_block(other_core, False)

    sel1 = sel[0, 1]
    sel2 = sel[0, 2]
    col1 = lax.rem(sel1, ROW)
    col2 = lax.rem(sel2, ROW)
    live1 = sel1 != ctx
    live2 = sel2 != ctx

    key_pos = lax.broadcasted_iota(jnp.int32, (HALF, BLOCK), 0)
    query_pos = lax.broadcasted_iota(jnp.int32, (HALF, BLOCK), 1)

    def forward_near(g):
        vt[0] = own[g, 1].T

        def one_head(r, _):
            hh = g * GROUP + r
            hcols = pl.ds(pl.multiple_of(hh * HD, HD), HD)
            q = qv[:, hcols]
            s = nt(own[g, 0, :HALF], q)
            s = jnp.where(key_pos <= query_pos, s, -1e30)
            late = nt(own[g, 0, HALF:], q[HALF:])
            late = jnp.where((key_pos <= query_pos)[:, :HALF], late, -1e30)
            top = jnp.max(s, axis=0, keepdims=True)
            top = jnp.concatenate(
                [top[:, :HALF], jnp.maximum(top[:, HALF:], jnp.max(late, axis=0, keepdims=True))], axis=1
            )
            shift = top * EXP2_SCALE
            e = jnp.exp2(s * EXP2_SCALE - shift)
            e2 = jnp.exp2(late * EXP2_SCALE - shift[:, HALF:])
            total = jnp.sum(e, axis=0, keepdims=True)
            total = jnp.concatenate(
                [total[:, :HALF], total[:, HALF:] + jnp.sum(e2, axis=0, keepdims=True)], axis=1
            )
            e = e.astype(BF16)
            e2 = e2.astype(BF16)
            eb[hh, 0:HALF, :] = e
            eb[hh, HALF:BLOCK, HALF:] = e2
            out = nn(vt[0, :, :HALF], e)
            out2 = nn(vt[0, :, HALF:], e2)
            ot[hcols, :] = jnp.concatenate([out[:, :HALF], out[:, HALF:] + out2], axis=1)
            top0[hh] = top
            total0[hh] = total
            return 0

        lax.fori_loop(0, GROUP, one_head, 0)

    def scores_far(g):
        w_ = win[g]

        def one_head(r, _):
            hh = g * GROUP + r
            hcols = pl.ds(pl.multiple_of(hh * HD, HD), HD)
            q = qv[:, hcols]
            first_top = top0[hh]
            top = first_top
            for j, (col, live) in enumerate(((col1, live1), (col2, live2))):
                for half in range(2):
                    s = nt(w_[0][col, half * HALF : (half + 1) * HALF], q)
                    sb[BLOCK * j + half * HALF : BLOCK * j + (half + 1) * HALF, :] = s
                    top = jnp.maximum(top, jnp.where(live, jnp.max(s, axis=0, keepdims=True), -1e30))
            shift = top * EXP2_SCALE
            fade = jnp.exp2(first_top * EXP2_SCALE - shift)
            total = total0[hh] * fade
            for j, live in enumerate((live1, live2)):
                sh = jnp.where(live, shift, 1e30)
                for half in range(2):
                    at = BLOCK * j + half * HALF
                    e = jnp.exp2(sb[at : at + HALF, :] * EXP2_SCALE - sh)
                    total = total + jnp.sum(e, axis=0, keepdims=True)
                    eb[hh, BLOCK + at : BLOCK + at + HALF, :] = e.astype(BF16)
            rl[hh] = 1.0 / total
            fades[hh] = fade
            return 0

        lax.fori_loop(0, GROUP, one_head, 0)

    def values_far(g):
        w_ = win[g]
        vt[1] = w_[1][col1].T
        vt[2] = w_[1][col2].T

        def one_head(r, _):
            hh = g * GROUP + r
            hcols = pl.ds(pl.multiple_of(hh * HD, HD), HD)
            out = ot[hcols, :] * fades[hh]
            out = out + nn(vt[1], eb[hh, BLOCK : 2 * BLOCK, :]) + nn(vt[2], eb[hh, 2 * BLOCK :, :])
            out = out * rl[hh]
            ot[hcols, :] = out
            ob[:, hcols] = out.T.astype(BF16)
            return 0

        lax.fori_loop(0, GROUP, one_head, 0, unroll=2)

    q_in.wait()
    for g in range(KV):
        forward_near(g)
    for g in range(KV):
        arrived(g, 0)
        scores_far(g)
    def project(block, cut, put, rows=slice(None)):
        def step(i, _):
            n0 = pl.multiple_of(i * 256, 256)
            cols = pl.ds(pl.multiple_of(block * WIDTH + cut * CUT + n0, 256), 256)
            put(pl.ds(n0, 256), nn(ob[:, rows], wv[rows, cols]))
            return 0

        lax.fori_loop(0, CUT // 256, step, 0)

    def hold(ref, cut):
        def put(cols, val):
            ref[cut, :, cols] = val

        return put

    early = slice(0, GROUP * HD)
    late = slice(GROUP * HD, WIDTH)
    arrived(0, 1)
    values_far(0)
    for j in range(CUTS):
        project(diagonal, j, hold(pdiag, j), early)
        project(other_chip, j, hold(pown, j), early)
    arrived(1, 1)
    values_far(1)

    def to_core(slot, cut):
        def put(cols, val):
            pcs[slot, cut, :, cols] = (val + pdiag[cut, :, cols] if slot == 0 else val).astype(BF16)

        return put

    def to_chip(cut):
        def put(cols, val):
            pxs[cut, :, cols] = (val + pown[cut, :, cols] + pcr[0, cut, :, cols].astype(F32)).astype(BF16)

        return put

    def keep(cut):
        def put(cols, val):
            pown[cut, :, cols] = val

        return put

    p_core = [
        [remote(pcs.at[i, j], pcr.at[i, j], pcss.at[i, j], pcrs.at[i, j], ctx, other_core) for j in range(CUTS)]
        for i in range(2)
    ]
    p_chip = [remote(pxs.at[j], pxr.at[j], pxss.at[j], pxrs.at[j], ctx, other_chip) for j in range(CUTS)]
    project(diagonal, 0, to_core(0, 0), late)
    p_core[0][0].start()
    project(diagonal, 1, to_core(0, 1), late)
    p_core[0][1].start()
    for j in range(CUTS):
        p_core[0][j].wait_recv()
        project(other_chip, j, to_chip(j), late)
        p_chip[j].start()
        if j == 0:
            for i in range(OG_CUTS):
                og_chip[i].wait_recv()
                og_pass[i].start()
    grad_block(other_chip, False)
    for i in range(OG_CUTS):
        og_pass[i].wait_recv()
    grad_block(diagonal, False)

    def back_tile(g, slot, w_, col, part, hh, q, do, rd, span):
        keys_at = slice(part * HALF, (part + 1) * HALF)
        e = eb[hh, slot * BLOCK + part * HALF : slot * BLOCK + (part + 1) * HALF, span]
        v = own[g, 1, keys_at] if slot == 0 else w_[1][col, keys_at]
        dp = nn(v, do)
        dsv = (e.astype(F32) * (dp - rd)).astype(BF16)
        acc[g, 0, slot, keys_at] += nn(dsv, q)
        return nn(kt[slot, :, keys_at], dsv)

    def value_far(g):
        for r in range(GROUP):
            hh = g * GROUP + r
            hcols = slice(hh * HD, (hh + 1) * HD)
            do32 = dot_[hcols, :] * rl[hh]
            do = do32.astype(BF16)
            rdb[hh] = jnp.sum(do32 * ot[hcols, :], axis=0, keepdims=True)
            dob[hcols, :] = do
            for slot in (1, 2):
                part = nt(eb[hh, slot * BLOCK : (slot + 1) * BLOCK, :], do)
                acc[g, 1, slot] = part if r == 0 else acc[g, 1, slot] + part

    def backward_far(g):
        w_ = win[g]
        kt[1] = w_[0][col1].T
        kt[2] = w_[0][col2].T
        acc[g, 0] = jnp.zeros(acc.shape[2:], F32)

        def one_head(r, _):
            hh = g * GROUP + r
            hcols = pl.ds(pl.multiple_of(hh * HD, HD), HD)
            q = qv[:, hcols]
            do = dob[hcols, :]
            rd = rdb[hh]
            dqt = jnp.zeros((HD, BLOCK), F32)
            for slot, col in ((1, col1), (2, col2)):
                for part in range(2):
                    dqt = dqt + back_tile(g, slot, w_, col, part, hh, q, do, rd, slice(None))
            dot_[hcols, :] = dqt
            return 0

        lax.fori_loop(0, GROUP, one_head, 0, unroll=GROUP)

    def backward_near(g):
        kt[0] = own[g, 0].T
        acc[g, 1, 0] = jnp.zeros((BLOCK, HD), F32)

        def one_head(r, _):
            hh = g * GROUP + r
            hcols = pl.ds(pl.multiple_of(hh * HD, HD), HD)
            q = qv[:, hcols]
            do = (dob[hcols, :].astype(F32) * fades[hh]).astype(BF16)
            rd = rdb[hh] * fades[hh]
            acc[g, 1, 0, :HALF] += nt(eb[hh, :HALF, :], do)
            acc[g, 1, 0, HALF:] += nt(eb[hh, HALF:BLOCK, HALF:], do[:, HALF:])
            dqt = dot_[hcols, :] + back_tile(g, 0, None, None, 0, hh, q, do, rd, slice(None))
            late = back_tile(g, 0, None, None, 1, hh, q[HALF:], do[:, HALF:], rd[:, HALF:], slice(HALF, BLOCK))
            dqt = jnp.concatenate([dqt[:, :HALF], dqt[:, HALF:] + late], axis=1)
            dqv[:, hcols] = (dqt * SCALE).T.astype(BF16)
            return 0

        lax.fori_loop(0, GROUP, one_head, 0, unroll=GROUP)

    give = [
        [
            [
                remote(
                    gs[g].at[lax.rem(y + ROW - k, ROW), part], gr[g].at[k - 1, part],
                    bds.at[g, part, k - 1], bdr.at[g, part, k - 1],
                    row_start + lax.rem(y + ROW - k, ROW), head,
                )
                for k in (1, 2, 3)
            ]
            for part in range(2)
        ]
        for g in range(KV)
    ]
    give_back = [
        [
            remote(gxs.at[g, part], gxr.at[g, part], bxs.at[g, part], bxr.at[g, part], preceding, head)
            for part in range(2)
        ]
        for g in range(KV)
    ]
    factors = (SCALE, 1.0)

    def send_grads(g, part):
        one = acc[g, part, 1] * factors[part]
        two = acc[g, part, 2] * factors[part]
        for c in range(ROW):
            gs[g][c, part] = (jnp.where(col1 == c, one, 0.0) + jnp.where(col2 == c, two, 0.0)).astype(BF16)
        for k in (1, 3, 2):
            give[g][part][k - 1].start()

    def sum_grads(g, part):
        for k in (1, 2, 3):
            give[g][part][k - 1].wait_recv()
        mine = None
        back = gs[g][y, part].astype(F32)
        for k in (1, 2, 3):
            came = gr[g][k - 1, part].astype(F32)
            inside = y + k < ROW
            kept = jnp.where(inside, came, 0.0)
            mine = kept if mine is None else mine + kept
            back = back + jnp.where(inside, 0.0, came)
        gxs[g, part] = back.astype(BF16)
        give_back[g][part].start()
        acc[g, part, 1] = mine

    outs = []

    def finish_grads(g, part):
        give_back[g][part].wait_recv()
        total = acc[g, part, 0] * factors[part] + acc[g, part, 1] + gxr[g, part].astype(F32)
        dkv_out[g, part] = total.astype(BF16)
        ref = (dk_hbm, dv_hbm)[part]
        cp = pltpu.make_async_copy(dkv_out.at[g, part], ref.at[:, pl.ds(g * HD, HD)], osem.at[2 * g + part])
        cp.start()
        outs.append(cp)

    for g in range(KV):
        value_far(g)
        send_grads(g, 1)
    for g in range(KV):
        backward_far(g)
        send_grads(g, 0)
    sum_grads(0, 1)
    backward_near(0)
    sum_grads(1, 1)
    backward_near(1)
    cp = pltpu.make_async_copy(dqv, dq_hbm, osem.at[4])
    cp.start()
    outs.append(cp)
    sum_grads(0, 0)
    for j in range(CUTS):
        project(other_core, j, to_core(1, j))
        p_core[1][j].start()
    for j in range(CUTS):
        project(head, j, keep(j))
    for j in range(CUTS):
        p_core[1][j].wait_recv()
        p_chip[j].wait()
        pxs[j] = (pown[j] + pcr[1, j].astype(F32) + pxr[j].astype(F32)).astype(BF16)
        cp = pltpu.make_async_copy(pxs.at[j], proj_hbm.at[:, pl.ds(j * CUT, CUT)], osem.at[5 + j])
        cp.start()
        outs.append(cp)
    sum_grads(1, 0)
    for g, part in ((0, 1), (1, 1), (0, 0), (1, 0)):
        finish_grads(g, part)

    og_core.wait_send()
    for i in range(OG_CUTS):
        og_chip[i].wait_send()
        og_pass[i].wait_send()
    for i in range(2):
        for j in range(CUTS):
            p_core[i][j].wait_send()
    for g in range(KV):
        for part in range(2):
            cross[g, part].wait_send()
            for k in (1, 2, 3):
                serve_own[g, part, k].wait_send()
            give_back[g][part].wait_send()
            for k in (1, 2, 3):
                give[g][part][k - 1].wait_send()
    for cp in outs:
        cp.wait()


def mover(*refs):
    ins, outs, held, sems = refs[:4], refs[4:8], refs[8:12], refs[12]
    copies = []
    for i, (n, first, rows) in enumerate(MOVES):
        at = pl.ds(first, rows)
        copies.append(
            (
                pltpu.make_async_copy(ins[n].at[at], held[n].at[at], sems.at[0, i]),
                pltpu.make_async_copy(held[n].at[at], outs[n].at[at], sems.at[1, i]),
            )
        )
    for come, _ in copies:
        come.start()
    for come, go in copies:
        come.wait()
        go.start()
    for _, go in copies:
        go.wait()


def local(queries, keys, values, selected, out_weight, out_grad):
    vm = pltpu.VMEM
    dma = pltpu.SemaphoreType.DMA
    anyspec = pl.BlockSpec(memory_space=pl.ANY)
    shapes = (
        jax.ShapeDtypeStruct((BLOCK, WIDTH), BF16),
        jax.ShapeDtypeStruct((BLOCK, WIDTH), BF16),
        jax.ShapeDtypeStruct((BLOCK, KV * HD), BF16),
        jax.ShapeDtypeStruct((BLOCK, KV * HD), BF16),
    )
    results = pl.pallas_call(
        kernel,
        out_shape=shapes,
        in_specs=[pl.BlockSpec(memory_space=pltpu.SMEM)] + [anyspec] * 5,
        out_specs=(anyspec,) * 4,
        scratch_shapes=[
            vm((KV, 2, BLOCK, HD), BF16),
            vm((ROW, BLOCK, HD), BF16),
            vm((ROW, BLOCK, HD), BF16),
            vm((ROW, BLOCK, HD), BF16),
            vm((ROW, BLOCK, HD), BF16),
            vm((3, HD, BLOCK), BF16),
            vm((3, HD, BLOCK), BF16),
            vm((BLOCK, WIDTH), BF16),
            vm((WIDTH, 4 * WIDTH), BF16),
            vm((4, BLOCK, WIDTH), BF16),
            vm((WIDTH, BLOCK), F32),
            vm((WIDTH, BLOCK), F32),
            vm((BLOCK, WIDTH), BF16),
            vm((KV * GROUP, 1, BLOCK), F32),
            vm((KV * GROUP, 3 * BLOCK, BLOCK), BF16),
            vm((2 * BLOCK, BLOCK), F32),
            vm((KV, 2, 3, BLOCK, HD), F32),
            vm((ROW, 2, BLOCK, HD), BF16),
            vm((ROW, 2, BLOCK, HD), BF16),
            vm((3, 2, BLOCK, HD), BF16),
            vm((3, 2, BLOCK, HD), BF16),
            vm((KV, 2, BLOCK, HD), BF16),
            vm((KV, 2, BLOCK, HD), BF16),
            vm((2, CUTS, BLOCK, CUT), BF16),
            vm((2, CUTS, BLOCK, CUT), BF16),
            vm((CUTS, BLOCK, CUT), BF16),
            vm((CUTS, BLOCK, CUT), BF16),
            vm((CUTS, BLOCK, CUT), F32),
            vm((BLOCK, WIDTH), BF16),
            vm((KV, 2, BLOCK, HD), BF16),
            vm((WIDTH, BLOCK), BF16),
            vm((KV * GROUP, 1, BLOCK), F32),
            vm((KV * GROUP, 1, BLOCK), F32),
            vm((KV * GROUP, 1, BLOCK), F32),
            vm((KV * GROUP, 1, BLOCK), F32),
            vm((CUTS, BLOCK, CUT), F32),
            dma((7,)), dma((5 + CUTS,)),
            dma((KV, 2)), dma((KV, 2)), dma((KV, 2, 3)), dma((KV, 2, 3)),
            dma((1,)), dma((1,)), dma((OG_CUTS,)), dma((OG_CUTS,)), dma((OG_CUTS,)), dma((OG_CUTS,)),
            dma((2, CUTS)), dma((2, CUTS)), dma((CUTS,)), dma((CUTS,)),
            dma((KV, 2, 3)), dma((KV, 2, 3)), dma((KV, 2)), dma((KV, 2)),
        ],
        compiler_params=pltpu.CompilerParams(
            collective_id=0, has_side_effects=True, vmem_limit_bytes=63 * 1024 * 1024
        ),
        cost_estimate=pl.CostEstimate(flops=18 * 10**9, bytes_accessed=16 * 2**20, transcendentals=6 * 10**6),
        name="layer",
    )(selected, queries, keys, values, out_weight, out_grad)
    return pl.pallas_call(
        mover,
        out_shape=shapes,
        in_specs=[anyspec] * 4,
        out_specs=(anyspec,) * 4,
        scratch_shapes=[vm(x.shape, x.dtype) for x in shapes] + [dma((2, len(MOVES)))],
        compiler_params=pltpu.CompilerParams(vmem_limit_bytes=60 * 1024 * 1024),
        name="move",
    )(*results)


def solution(mesh):
    placed = (
        P("ctx", "head"),
        P("ctx", "head"),
        P("ctx", "head"),
        P("ctx", None),
        P("head", None),
        P("ctx", "head"),
    )
    return jax.shard_map(
        local,
        mesh=mesh,
        in_specs=placed,
        out_specs=(P("ctx", "head"), P("ctx", "head"), P("ctx", "head"), P("ctx", "head")),
        check_vma=False,
    )
```

```python
import functools
import math

import jax
import jax.numpy as jnp
from jax import lax
from jax.experimental import pallas as pl
from jax.experimental.pallas import tpu as pltpu
from jax.sharding import PartitionSpec as P

HD = 128
BLOCK = 512
HALF = BLOCK // 2
WIDTH = 1024
GROUP = 4
KV = 2
ROW = 4
MESH = pl.DeviceIdType.MESH
SCALE = 1.0 / math.sqrt(HD)
EXP2_SCALE = SCALE * math.log2(math.e)
BF16 = jnp.bfloat16
F32 = jnp.float32
OG_CUTS = 2
OG_ROWS = BLOCK // OG_CUTS
CUTS = 2
CUT = WIDTH // CUTS
MOVES = [(n, i * 128, 128) for n in (0, 1) for i in range(4)] + [(n, i * 256, 256) for n in (2, 3) for i in range(2)]


def nn(a, b):
    return lax.dot_general(a, b, (((1,), (0,)), ((), ())), preferred_element_type=F32)


def nt(a, b):
    return lax.dot_general(a, b, (((1,), (1,)), ((), ())), preferred_element_type=F32)


def kernel(
    sel, q_hbm, k_hbm, v_hbm, w_hbm, og_hbm,
    proj_hbm, dq_hbm, dk_hbm, dv_hbm,
    own, wink0, winv0, wink1, winv1, vt, kt, qv, wv, ogb, dot_, ot, ob, rl, eb, sb, acc,
    gs0, gs1, gr0, gr1, gxs, gxr, pcs, pcr, pxs, pxr, pown, dqv, dkv_out, dob, rdb, top0, total0, fades, pdiag,
    lsem, osem, xs, xr, ds_, dr, ocs, ocr, oxs, oxr, ofs, ofr, pcss, pcrs, pxss, pxrs, bds, bdr, bxs, bxr,
):
    win = ((wink0, winv0), (wink1, winv1))
    gs = (gs0, gs1)
    gr = (gr0, gr1)
    ctx = lax.axis_index("ctx")
    head = lax.axis_index("head")
    y = lax.rem(ctx, ROW)
    row_start = ctx - y
    following = lax.rem(ctx + ROW, 32)
    preceding = lax.rem(ctx + 32 - ROW, 32)
    chip = head // 2
    core = lax.rem(head, 2)
    other_core = chip * 2 + 1 - core
    other_chip = (1 - chip) * 2 + core
    diagonal = (1 - chip) * 2 + 1 - core

    def peer(k):
        return row_start + lax.rem(y + k, ROW)

    def remote(src, dst, ss, rs, c, h):
        return pltpu.make_async_remote_copy(
            src_ref=src, dst_ref=dst, send_sem=ss, recv_sem=rs, device_id=(c, h), device_id_type=MESH
        )

    kv_in = []
    for g in range(KV):
        cols = pl.ds(g * HD, HD)
        kv_in.append(
            (
                pltpu.make_async_copy(k_hbm.at[:, cols], own.at[g, 0], lsem.at[2 * g]),
                pltpu.make_async_copy(v_hbm.at[:, cols], own.at[g, 1], lsem.at[2 * g + 1]),
            )
        )
        kv_in[g][0].start()
        kv_in[g][1].start()
    og_in = pltpu.make_async_copy(og_hbm, ogb.at[head], lsem.at[4])
    og_in.start()
    w_in = pltpu.make_async_copy(w_hbm, wv, lsem.at[5])
    w_in.start()
    q_in = pltpu.make_async_copy(q_hbm, qv, lsem.at[6])
    q_in.start()

    barrier = pltpu.get_barrier_semaphore()
    for c, h in (
        (following, head), (preceding, head), (peer(1), head), (peer(2), head), (peer(3), head),
        (ctx, other_core), (ctx, other_chip),
    ):
        pl.semaphore_signal(barrier, inc=1, device_id=(c, h), device_id_type=MESH)
    pl.semaphore_wait(barrier, 7)

    pieces = [(g, part) for part in range(2) for g in range(KV)]
    cross = {
        (g, p): remote(own.at[g, p], win[g][p].at[y], xs.at[g, p], xr.at[g, p], following, head) for g, p in pieces
    }
    serve_own = {
        (g, p, k): remote(own.at[g, p], win[g][p].at[y], ds_.at[g, p, k - 1], dr.at[g, p, k - 1], peer(k), head)
        for g, p in pieces
        for k in (1, 2, 3)
    }
    serve_prev = {
        (g, p, k): remote(win[g][p].at[y], win[g][p].at[y], ds_.at[g, p, k - 1], dr.at[g, p, k - 1], peer(k), head)
        for g, p in pieces
        for k in (1, 2, 3)
    }

    def start_own(g, p):
        for k in (1, 3, 2):
            pl.when(y + k < ROW)(serve_own[g, p, k].start)

    def pass_on(g, p):
        cross[g, p].wait_recv()
        for k in (3, 1, 2):
            pl.when(y + k >= ROW)(serve_prev[g, p, k].start)

    def arrived(g, p):
        for k in (1, 2, 3):
            serve_own[g, p, k].wait_recv()

    for g, p in pieces:
        kv_in[g][p].wait()
        cross[g, p].start()
        if p == 0:
            start_own(g, p)

    og_in.wait()
    og_core = remote(ogb.at[head], ogb.at[head], ocs.at[0], ocr.at[0], ctx, other_core)
    og_core.start()
    og_chip = []
    og_pass = []
    for i in range(OG_CUTS):
        rows = pl.ds(i * OG_ROWS, OG_ROWS)
        og_chip.append(
            remote(ogb.at[head, rows], ogb.at[head, rows], oxs.at[i], oxr.at[i], ctx, other_chip)
        )
        og_pass.append(
            remote(ogb.at[other_chip, rows], ogb.at[other_chip, rows], ofs.at[i], ofr.at[i], ctx, other_core)
        )

    def grad_block(block, first):
        cols = pl.ds(pl.multiple_of(block * WIDTH, WIDTH), WIDTH)

        def step(i, _):
            rows = pl.ds(pl.multiple_of(i * 256, 256), 256)
            part = nt(wv[rows, cols], ogb[block])
            dot_[rows, :] = part if first else dot_[rows, :] + part
            return 0

        lax.fori_loop(0, WIDTH // 256, step, 0)

    w_in.wait()
    grad_block(head, True)

    pass_on(0, 0)
    pass_on(1, 0)
    start_own(0, 1)
    pass_on(0, 1)
    start_own(1, 1)
    pass_on(1, 1)
    for i in range(OG_CUTS):
        og_chip[i].start()
    og_core.wait_recv()
    grad_block(other_core, False)

    sel1 = sel[0, 1]
    sel2 = sel[0, 2]
    col1 = lax.rem(sel1, ROW)
    col2 = lax.rem(sel2, ROW)
    live1 = sel1 != ctx
    live2 = sel2 != ctx

    key_pos = lax.broadcasted_iota(jnp.int32, (HALF, BLOCK), 0)
    query_pos = lax.broadcasted_iota(jnp.int32, (HALF, BLOCK), 1)

    def forward_near(g):
        vt[0] = own[g, 1].T

        def one_head(r, _):
            hh = g * GROUP + r
            hcols = pl.ds(pl.multiple_of(hh * HD, HD), HD)
            q = qv[:, hcols]
            s = nt(own[g, 0, :HALF], q)
            s = jnp.where(key_pos <= query_pos, s, -1e30)
            late = nt(own[g, 0, HALF:], q[HALF:])
            late = jnp.where((key_pos <= query_pos)[:, :HALF], late, -1e30)
            top = jnp.max(s, axis=0, keepdims=True)
            top = jnp.concatenate(
                [top[:, :HALF], jnp.maximum(top[:, HALF:], jnp.max(late, axis=0, keepdims=True))], axis=1
            )
            shift = top * EXP2_SCALE
            e = jnp.exp2(s * EXP2_SCALE - shift)
            e2 = jnp.exp2(late * EXP2_SCALE - shift[:, HALF:])
            total = jnp.sum(e, axis=0, keepdims=True)
            total = jnp.concatenate(
                [total[:, :HALF], total[:, HALF:] + jnp.sum(e2, axis=0, keepdims=True)], axis=1
            )
            e = e.astype(BF16)
            e2 = e2.astype(BF16)
            eb[hh, 0:HALF, :] = e
            eb[hh, HALF:BLOCK, HALF:] = e2
            out = nn(vt[0, :, :HALF], e)
            out2 = nn(vt[0, :, HALF:], e2)
            ot[hcols, :] = jnp.concatenate([out[:, :HALF], out[:, HALF:] + out2], axis=1)
            top0[hh] = top
            total0[hh] = total
            return 0

        lax.fori_loop(0, GROUP, one_head, 0)

    def scores_far(g):
        w_ = win[g]

        def one_head(r, _):
            hh = g * GROUP + r
            hcols = pl.ds(pl.multiple_of(hh * HD, HD), HD)
            q = qv[:, hcols]
            first_top = top0[hh]
            top = first_top
            for j, (col, live) in enumerate(((col1, live1), (col2, live2))):
                for half in range(2):
                    s = nt(w_[0][col, half * HALF : (half + 1) * HALF], q)
                    sb[BLOCK * j + half * HALF : BLOCK * j + (half + 1) * HALF, :] = s
                    top = jnp.maximum(top, jnp.where(live, jnp.max(s, axis=0, keepdims=True), -1e30))
            shift = top * EXP2_SCALE
            fade = jnp.exp2(first_top * EXP2_SCALE - shift)
            total = total0[hh] * fade
            for j, live in enumerate((live1, live2)):
                sh = jnp.where(live, shift, 1e30)
                for half in range(2):
                    at = BLOCK * j + half * HALF
                    e = jnp.exp2(sb[at : at + HALF, :] * EXP2_SCALE - sh)
                    total = total + jnp.sum(e, axis=0, keepdims=True)
                    eb[hh, BLOCK + at : BLOCK + at + HALF, :] = e.astype(BF16)
            rl[hh] = 1.0 / total
            fades[hh] = fade
            return 0

        lax.fori_loop(0, GROUP, one_head, 0)

    def values_far(g):
        w_ = win[g]
        vt[1] = w_[1][col1].T
        vt[2] = w_[1][col2].T

        def one_head(r, _):
            hh = g * GROUP + r
            hcols = pl.ds(pl.multiple_of(hh * HD, HD), HD)
            out = ot[hcols, :] * fades[hh]
            out = out + nn(vt[1], eb[hh, BLOCK : 2 * BLOCK, :]) + nn(vt[2], eb[hh, 2 * BLOCK :, :])
            out = out * rl[hh]
            ot[hcols, :] = out
            ob[:, hcols] = out.T.astype(BF16)
            return 0

        lax.fori_loop(0, GROUP, one_head, 0, unroll=2)

    q_in.wait()
    for g in range(KV):
        forward_near(g)
    for g in range(KV):
        arrived(g, 0)
        scores_far(g)
    def project(block, cut, put, rows=slice(None)):
        def step(i, _):
            n0 = pl.multiple_of(i * 256, 256)
            cols = pl.ds(pl.multiple_of(block * WIDTH + cut * CUT + n0, 256), 256)
            put(pl.ds(n0, 256), nn(ob[:, rows], wv[rows, cols]))
            return 0

        lax.fori_loop(0, CUT // 256, step, 0)

    def hold(ref, cut):
        def put(cols, val):
            ref[cut, :, cols] = val

        return put

    early = slice(0, GROUP * HD)
    late = slice(GROUP * HD, WIDTH)
    arrived(0, 1)
    values_far(0)
    for j in range(CUTS):
        project(diagonal, j, hold(pdiag, j), early)
        project(other_chip, j, hold(pown, j), early)
    arrived(1, 1)
    values_far(1)

    def to_core(slot, cut):
        def put(cols, val):
            pcs[slot, cut, :, cols] = (val + pdiag[cut, :, cols] if slot == 0 else val).astype(BF16)

        return put

    def to_chip(cut):
        def put(cols, val):
            pxs[cut, :, cols] = (val + pown[cut, :, cols] + pcr[0, cut, :, cols].astype(F32)).astype(BF16)

        return put

    def keep(cut):
        def put(cols, val):
            pown[cut, :, cols] = val

        return put

    p_core = [
        [remote(pcs.at[i, j], pcr.at[i, j], pcss.at[i, j], pcrs.at[i, j], ctx, other_core) for j in range(CUTS)]
        for i in range(2)
    ]
    p_chip = [remote(pxs.at[j], pxr.at[j], pxss.at[j], pxrs.at[j], ctx, other_chip) for j in range(CUTS)]
    project(diagonal, 0, to_core(0, 0), late)
    p_core[0][0].start()
    project(diagonal, 1, to_core(0, 1), late)
    p_core[0][1].start()
    for j in range(CUTS):
        p_core[0][j].wait_recv()
        project(other_chip, j, to_chip(j), late)
        p_chip[j].start()
        if j == 0:
            for i in range(OG_CUTS):
                og_chip[i].wait_recv()
                og_pass[i].start()
    grad_block(other_chip, False)
    for i in range(OG_CUTS):
        og_pass[i].wait_recv()
    grad_block(diagonal, False)

    def back_tile(g, slot, w_, col, part, hh, q, do, rd, span):
        keys_at = slice(part * HALF, (part + 1) * HALF)
        e = eb[hh, slot * BLOCK + part * HALF : slot * BLOCK + (part + 1) * HALF, span]
        v = own[g, 1, keys_at] if slot == 0 else w_[1][col, keys_at]
        dp = nn(v, do)
        dsv = (e.astype(F32) * (dp - rd)).astype(BF16)
        acc[g, 0, slot, keys_at] += nn(dsv, q)
        return nn(kt[slot, :, keys_at], dsv)

    def value_far(g):
        for r in range(GROUP):
            hh = g * GROUP + r
            hcols = slice(hh * HD, (hh + 1) * HD)
            do32 = dot_[hcols, :] * rl[hh]
            do = do32.astype(BF16)
            rdb[hh] = jnp.sum(do32 * ot[hcols, :], axis=0, keepdims=True)
            dob[hcols, :] = do
            for slot in (1, 2):
                part = nt(eb[hh, slot * BLOCK : (slot + 1) * BLOCK, :], do)
                acc[g, 1, slot] = part if r == 0 else acc[g, 1, slot] + part

    def backward_far(g):
        w_ = win[g]
        kt[1] = w_[0][col1].T
        kt[2] = w_[0][col2].T
        acc[g, 0] = jnp.zeros(acc.shape[2:], F32)

        def one_head(r, _):
            hh = g * GROUP + r
            hcols = pl.ds(pl.multiple_of(hh * HD, HD), HD)
            q = qv[:, hcols]
            do = dob[hcols, :]
            rd = rdb[hh]
            dqt = jnp.zeros((HD, BLOCK), F32)
            for slot, col in ((1, col1), (2, col2)):
                for part in range(2):
                    dqt = dqt + back_tile(g, slot, w_, col, part, hh, q, do, rd, slice(None))
            dot_[hcols, :] = dqt
            return 0

        lax.fori_loop(0, GROUP, one_head, 0, unroll=GROUP)

    def backward_near(g):
        kt[0] = own[g, 0].T
        acc[g, 1, 0] = jnp.zeros((BLOCK, HD), F32)

        def one_head(r, _):
            hh = g * GROUP + r
            hcols = pl.ds(pl.multiple_of(hh * HD, HD), HD)
            q = qv[:, hcols]
            do = (dob[hcols, :].astype(F32) * fades[hh]).astype(BF16)
            rd = rdb[hh] * fades[hh]
            acc[g, 1, 0, :HALF] += nt(eb[hh, :HALF, :], do)
            acc[g, 1, 0, HALF:] += nt(eb[hh, HALF:BLOCK, HALF:], do[:, HALF:])
            dqt = dot_[hcols, :] + back_tile(g, 0, None, None, 0, hh, q, do, rd, slice(None))
            late = back_tile(g, 0, None, None, 1, hh, q[HALF:], do[:, HALF:], rd[:, HALF:], slice(HALF, BLOCK))
            dqt = jnp.concatenate([dqt[:, :HALF], dqt[:, HALF:] + late], axis=1)
            dqv[:, hcols] = (dqt * SCALE).T.astype(BF16)
            return 0

        lax.fori_loop(0, GROUP, one_head, 0, unroll=GROUP)

    give = [
        [
            [
                remote(
                    gs[g].at[lax.rem(y + ROW - k, ROW), part], gr[g].at[k - 1, part],
                    bds.at[g, part, k - 1], bdr.at[g, part, k - 1],
                    row_start + lax.rem(y + ROW - k, ROW), head,
                )
                for k in (1, 2, 3)
            ]
            for part in range(2)
        ]
        for g in range(KV)
    ]
    give_back = [
        [
            remote(gxs.at[g, part], gxr.at[g, part], bxs.at[g, part], bxr.at[g, part], preceding, head)
            for part in range(2)
        ]
        for g in range(KV)
    ]
    factors = (SCALE, 1.0)

    def send_grads(g, part):
        one = acc[g, part, 1] * factors[part]
        two = acc[g, part, 2] * factors[part]
        for c in range(ROW):
            gs[g][c, part] = (jnp.where(col1 == c, one, 0.0) + jnp.where(col2 == c, two, 0.0)).astype(BF16)
        for k in (1, 3, 2):
            give[g][part][k - 1].start()

    def sum_grads(g, part):
        for k in (1, 2, 3):
            give[g][part][k - 1].wait_recv()
        mine = None
        back = gs[g][y, part].astype(F32)
        for k in (1, 2, 3):
            came = gr[g][k - 1, part].astype(F32)
            inside = y + k < ROW
            kept = jnp.where(inside, came, 0.0)
            mine = kept if mine is None else mine + kept
            back = back + jnp.where(inside, 0.0, came)
        gxs[g, part] = back.astype(BF16)
        give_back[g][part].start()
        acc[g, part, 1] = mine

    outs = []

    def finish_grads(g, part):
        give_back[g][part].wait_recv()
        total = acc[g, part, 0] * factors[part] + acc[g, part, 1] + gxr[g, part].astype(F32)
        dkv_out[g, part] = total.astype(BF16)
        ref = (dk_hbm, dv_hbm)[part]
        cp = pltpu.make_async_copy(dkv_out.at[g, part], ref.at[:, pl.ds(g * HD, HD)], osem.at[2 * g + part])
        cp.start()
        outs.append(cp)

    for g in range(KV):
        value_far(g)
        send_grads(g, 1)
    for g in range(KV):
        backward_far(g)
        send_grads(g, 0)
    sum_grads(0, 1)
    backward_near(0)
    sum_grads(1, 1)
    backward_near(1)
    cp = pltpu.make_async_copy(dqv, dq_hbm, osem.at[4])
    cp.start()
    outs.append(cp)
    sum_grads(0, 0)
    for j in range(CUTS):
        project(other_core, j, to_core(1, j))
        p_core[1][j].start()
    for j in range(CUTS):
        project(head, j, keep(j))
    sum_grads(1, 0)
    for j in range(CUTS):
        p_core[1][j].wait_recv()
        p_chip[j].wait()
        pxs[j] = (pown[j] + pcr[1, j].astype(F32) + pxr[j].astype(F32)).astype(BF16)
        cp = pltpu.make_async_copy(pxs.at[j], proj_hbm.at[:, pl.ds(j * CUT, CUT)], osem.at[5 + j])
        cp.start()
        outs.append(cp)
    for g, part in ((0, 1), (1, 1), (0, 0), (1, 0)):
        finish_grads(g, part)

    og_core.wait_send()
    for i in range(OG_CUTS):
        og_chip[i].wait_send()
        og_pass[i].wait_send()
    for i in range(2):
        for j in range(CUTS):
            p_core[i][j].wait_send()
    for g in range(KV):
        for part in range(2):
            cross[g, part].wait_send()
            for k in (1, 2, 3):
                serve_own[g, part, k].wait_send()
            give_back[g][part].wait_send()
            for k in (1, 2, 3):
                give[g][part][k - 1].wait_send()
    for cp in outs:
        cp.wait()


def mover(*refs):
    ins, outs, held, sems = refs[:4], refs[4:8], refs[8:12], refs[12]
    copies = []
    for i, (n, first, rows) in enumerate(MOVES):
        at = pl.ds(first, rows)
        copies.append(
            (
                pltpu.make_async_copy(ins[n].at[at], held[n].at[at], sems.at[0, i]),
                pltpu.make_async_copy(held[n].at[at], outs[n].at[at], sems.at[1, i]),
            )
        )
    for come, _ in copies:
        come.start()
    for come, go in copies:
        come.wait()
        go.start()
    for _, go in copies:
        go.wait()


def local(queries, keys, values, selected, out_weight, out_grad):
    vm = pltpu.VMEM
    dma = pltpu.SemaphoreType.DMA
    anyspec = pl.BlockSpec(memory_space=pl.ANY)
    shapes = (
        jax.ShapeDtypeStruct((BLOCK, WIDTH), BF16),
        jax.ShapeDtypeStruct((BLOCK, WIDTH), BF16),
        jax.ShapeDtypeStruct((BLOCK, KV * HD), BF16),
        jax.ShapeDtypeStruct((BLOCK, KV * HD), BF16),
    )
    results = pl.pallas_call(
        kernel,
        out_shape=shapes,
        in_specs=[pl.BlockSpec(memory_space=pltpu.SMEM)] + [anyspec] * 5,
        out_specs=(anyspec,) * 4,
        scratch_shapes=[
            vm((KV, 2, BLOCK, HD), BF16),
            vm((ROW, BLOCK, HD), BF16),
            vm((ROW, BLOCK, HD), BF16),
            vm((ROW, BLOCK, HD), BF16),
            vm((ROW, BLOCK, HD), BF16),
            vm((3, HD, BLOCK), BF16),
            vm((3, HD, BLOCK), BF16),
            vm((BLOCK, WIDTH), BF16),
            vm((WIDTH, 4 * WIDTH), BF16),
            vm((4, BLOCK, WIDTH), BF16),
            vm((WIDTH, BLOCK), F32),
            vm((WIDTH, BLOCK), F32),
            vm((BLOCK, WIDTH), BF16),
            vm((KV * GROUP, 1, BLOCK), F32),
            vm((KV * GROUP, 3 * BLOCK, BLOCK), BF16),
            vm((2 * BLOCK, BLOCK), F32),
            vm((KV, 2, 3, BLOCK, HD), F32),
            vm((ROW, 2, BLOCK, HD), BF16),
            vm((ROW, 2, BLOCK, HD), BF16),
            vm((3, 2, BLOCK, HD), BF16),
            vm((3, 2, BLOCK, HD), BF16),
            vm((KV, 2, BLOCK, HD), BF16),
            vm((KV, 2, BLOCK, HD), BF16),
            vm((2, CUTS, BLOCK, CUT), BF16),
            vm((2, CUTS, BLOCK, CUT), BF16),
            vm((CUTS, BLOCK, CUT), BF16),
            vm((CUTS, BLOCK, CUT), BF16),
            vm((CUTS, BLOCK, CUT), F32),
            vm((BLOCK, WIDTH), BF16),
            vm((KV, 2, BLOCK, HD), BF16),
            vm((WIDTH, BLOCK), BF16),
            vm((KV * GROUP, 1, BLOCK), F32),
            vm((KV * GROUP, 1, BLOCK), F32),
            vm((KV * GROUP, 1, BLOCK), F32),
            vm((KV * GROUP, 1, BLOCK), F32),
            vm((CUTS, BLOCK, CUT), F32),
            dma((7,)), dma((5 + CUTS,)),
            dma((KV, 2)), dma((KV, 2)), dma((KV, 2, 3)), dma((KV, 2, 3)),
            dma((1,)), dma((1,)), dma((OG_CUTS,)), dma((OG_CUTS,)), dma((OG_CUTS,)), dma((OG_CUTS,)),
            dma((2, CUTS)), dma((2, CUTS)), dma((CUTS,)), dma((CUTS,)),
            dma((KV, 2, 3)), dma((KV, 2, 3)), dma((KV, 2)), dma((KV, 2)),
        ],
        compiler_params=pltpu.CompilerParams(
            collective_id=0, has_side_effects=True, vmem_limit_bytes=63 * 1024 * 1024
        ),
        cost_estimate=pl.CostEstimate(flops=18 * 10**9, bytes_accessed=16 * 2**20, transcendentals=6 * 10**6),
        name="layer",
    )(selected, queries, keys, values, out_weight, out_grad)
    return pl.pallas_call(
        mover,
        out_shape=shapes,
        in_specs=[anyspec] * 4,
        out_specs=(anyspec,) * 4,
        scratch_shapes=[vm(x.shape, x.dtype) for x in shapes] + [dma((2, len(MOVES)))],
        compiler_params=pltpu.CompilerParams(vmem_limit_bytes=60 * 1024 * 1024),
        name="move",
    )(*results)


def solution(mesh):
    placed = (
        P("ctx", "head"),
        P("ctx", "head"),
        P("ctx", "head"),
        P("ctx", None),
        P("head", None),
        P("ctx", "head"),
    )
    return jax.shard_map(
        local,
        mesh=mesh,
        in_specs=placed,
        out_specs=(P("ctx", "head"), P("ctx", "head"), P("ctx", "head"), P("ctx", "head")),
        check_vma=False,
    )
```

```python
import functools
import math

import jax
import jax.numpy as jnp
from jax import lax
from jax.experimental import pallas as pl
from jax.experimental.pallas import tpu as pltpu
from jax.sharding import PartitionSpec as P

HD = 128
BLOCK = 512
HALF = BLOCK // 2
WIDTH = 1024
GROUP = 4
KV = 2
ROW = 4
MESH = pl.DeviceIdType.MESH
SCALE = 1.0 / math.sqrt(HD)
EXP2_SCALE = SCALE * math.log2(math.e)
BF16 = jnp.bfloat16
F32 = jnp.float32
OG_CUTS = 2
OG_ROWS = BLOCK // OG_CUTS
CUTS = 2
CUT = WIDTH // CUTS
MOVES = [(n, i * 128, 128) for n in (0, 1) for i in range(4)] + [(n, i * 256, 256) for n in (2, 3) for i in range(2)]


def nn(a, b):
    return lax.dot_general(a, b, (((1,), (0,)), ((), ())), preferred_element_type=F32)


def nt(a, b):
    return lax.dot_general(a, b, (((1,), (1,)), ((), ())), preferred_element_type=F32)


def kernel(
    sel, q_hbm, k_hbm, v_hbm, w_hbm, og_hbm,
    proj_hbm, dq_hbm, dk_hbm, dv_hbm,
    own, wink0, winv0, wink1, winv1, vt, kt, qv, wv, ogb, dot_, ot, ob, rl, eb, sb, acc,
    gs0, gs1, gr0, gr1, gxs, gxr, pcs, pcr, pxs, pxr, pown, dqv, dkv_out, dob, rdb, top0, total0, fades, pdiag,
    lsem, osem, xs, xr, ds_, dr, ocs, ocr, oxs, oxr, ofs, ofr, pcss, pcrs, pxss, pxrs, bds, bdr, bxs, bxr,
):
    win = ((wink0, winv0), (wink1, winv1))
    gs = (gs0, gs1)
    gr = (gr0, gr1)
    ctx = lax.axis_index("ctx")
    head = lax.axis_index("head")
    y = lax.rem(ctx, ROW)
    row_start = ctx - y
    following = lax.rem(ctx + ROW, 32)
    preceding = lax.rem(ctx + 32 - ROW, 32)
    chip = head // 2
    core = lax.rem(head, 2)
    other_core = chip * 2 + 1 - core
    other_chip = (1 - chip) * 2 + core
    diagonal = (1 - chip) * 2 + 1 - core

    def peer(k):
        return row_start + lax.rem(y + k, ROW)

    def remote(src, dst, ss, rs, c, h):
        return pltpu.make_async_remote_copy(
            src_ref=src, dst_ref=dst, send_sem=ss, recv_sem=rs, device_id=(c, h), device_id_type=MESH
        )

    kv_in = []
    for g in range(KV):
        cols = pl.ds(g * HD, HD)
        kv_in.append(
            (
                pltpu.make_async_copy(k_hbm.at[:, cols], own.at[g, 0], lsem.at[2 * g]),
                pltpu.make_async_copy(v_hbm.at[:, cols], own.at[g, 1], lsem.at[2 * g + 1]),
            )
        )
        kv_in[g][0].start()
        kv_in[g][1].start()
    og_in = pltpu.make_async_copy(og_hbm, ogb.at[head], lsem.at[4])
    og_in.start()
    w_in = pltpu.make_async_copy(w_hbm, wv, lsem.at[5])
    w_in.start()
    q_in = pltpu.make_async_copy(q_hbm, qv, lsem.at[6])
    q_in.start()

    barrier = pltpu.get_barrier_semaphore()
    for c, h in (
        (following, head), (preceding, head), (peer(1), head), (peer(2), head), (peer(3), head),
        (ctx, other_core), (ctx, other_chip),
    ):
        pl.semaphore_signal(barrier, inc=1, device_id=(c, h), device_id_type=MESH)
    pl.semaphore_wait(barrier, 7)

    pieces = [(g, part) for part in range(2) for g in range(KV)]
    cross = {
        (g, p): remote(own.at[g, p], win[g][p].at[y], xs.at[g, p], xr.at[g, p], following, head) for g, p in pieces
    }
    serve_own = {
        (g, p, k): remote(own.at[g, p], win[g][p].at[y], ds_.at[g, p, k - 1], dr.at[g, p, k - 1], peer(k), head)
        for g, p in pieces
        for k in (1, 2, 3)
    }
    serve_prev = {
        (g, p, k): remote(win[g][p].at[y], win[g][p].at[y], ds_.at[g, p, k - 1], dr.at[g, p, k - 1], peer(k), head)
        for g, p in pieces
        for k in (1, 2, 3)
    }

    def start_own(g, p):
        for k in (1, 3, 2):
            pl.when(y + k < ROW)(serve_own[g, p, k].start)

    def pass_on(g, p):
        cross[g, p].wait_recv()
        for k in (3, 1, 2):
            pl.when(y + k >= ROW)(serve_prev[g, p, k].start)

    def arrived(g, p):
        for k in (1, 2, 3):
            serve_own[g, p, k].wait_recv()

    for g, p in pieces:
        kv_in[g][p].wait()
        cross[g, p].start()
        if p == 0:
            start_own(g, p)

    og_in.wait()
    og_core = remote(ogb.at[head], ogb.at[head], ocs.at[0], ocr.at[0], ctx, other_core)
    og_core.start()
    og_chip = []
    og_pass = []
    for i in range(OG_CUTS):
        rows = pl.ds(i * OG_ROWS, OG_ROWS)
        og_chip.append(
            remote(ogb.at[head, rows], ogb.at[head, rows], oxs.at[i], oxr.at[i], ctx, other_chip)
        )
        og_pass.append(
            remote(ogb.at[other_chip, rows], ogb.at[other_chip, rows], ofs.at[i], ofr.at[i], ctx, other_core)
        )

    def grad_block(block, first, start=0, stop=WIDTH // 256):
        cols = pl.ds(pl.multiple_of(block * WIDTH, WIDTH), WIDTH)

        def step(i, _):
            rows = pl.ds(pl.multiple_of(i * 256, 256), 256)
            part = nt(wv[rows, cols], ogb[block])
            dot_[rows, :] = part if first else dot_[rows, :] + part
            return 0

        lax.fori_loop(start, stop, step, 0)

    w_in.wait()
    grad_block(head, True)

    pass_on(0, 0)
    pass_on(1, 0)
    start_own(0, 1)
    pass_on(0, 1)
    start_own(1, 1)
    pass_on(1, 1)
    for i in range(OG_CUTS):
        og_chip[i].start()
    og_core.wait_recv()
    grad_block(other_core, False)

    sel1 = sel[0, 1]
    sel2 = sel[0, 2]
    col1 = lax.rem(sel1, ROW)
    col2 = lax.rem(sel2, ROW)
    live1 = sel1 != ctx
    live2 = sel2 != ctx

    key_pos = lax.broadcasted_iota(jnp.int32, (HALF, BLOCK), 0)
    query_pos = lax.broadcasted_iota(jnp.int32, (HALF, BLOCK), 1)

    def forward_near(g):
        vt[0] = own[g, 1].T

        def one_head(r, _):
            hh = g * GROUP + r
            hcols = pl.ds(pl.multiple_of(hh * HD, HD), HD)
            q = qv[:, hcols]
            s = nt(own[g, 0, :HALF], q)
            s = jnp.where(key_pos <= query_pos, s, -1e30)
            late = nt(own[g, 0, HALF:], q[HALF:])
            late = jnp.where((key_pos <= query_pos)[:, :HALF], late, -1e30)
            top = jnp.max(s, axis=0, keepdims=True)
            top = jnp.concatenate(
                [top[:, :HALF], jnp.maximum(top[:, HALF:], jnp.max(late, axis=0, keepdims=True))], axis=1
            )
            shift = top * EXP2_SCALE
            e = jnp.exp2(s * EXP2_SCALE - shift)
            e2 = jnp.exp2(late * EXP2_SCALE - shift[:, HALF:])
            total = jnp.sum(e, axis=0, keepdims=True)
            total = jnp.concatenate(
                [total[:, :HALF], total[:, HALF:] + jnp.sum(e2, axis=0, keepdims=True)], axis=1
            )
            e = e.astype(BF16)
            e2 = e2.astype(BF16)
            eb[hh, 0:HALF, :] = e
            eb[hh, HALF:BLOCK, HALF:] = e2
            out = nn(vt[0, :, :HALF], e)
            out2 = nn(vt[0, :, HALF:], e2)
            ot[hcols, :] = jnp.concatenate([out[:, :HALF], out[:, HALF:] + out2], axis=1)
            top0[hh] = top
            total0[hh] = total
            return 0

        lax.fori_loop(0, GROUP, one_head, 0)

    def scores_far(g):
        w_ = win[g]

        def one_head(r, _):
            hh = g * GROUP + r
            hcols = pl.ds(pl.multiple_of(hh * HD, HD), HD)
            q = qv[:, hcols]
            first_top = top0[hh]
            top = first_top
            for j, (col, live) in enumerate(((col1, live1), (col2, live2))):
                for half in range(2):
                    s = nt(w_[0][col, half * HALF : (half + 1) * HALF], q)
                    sb[BLOCK * j + half * HALF : BLOCK * j + (half + 1) * HALF, :] = s
                    top = jnp.maximum(top, jnp.where(live, jnp.max(s, axis=0, keepdims=True), -1e30))
            shift = top * EXP2_SCALE
            fade = jnp.exp2(first_top * EXP2_SCALE - shift)
            total = total0[hh] * fade
            for j, live in enumerate((live1, live2)):
                sh = jnp.where(live, shift, 1e30)
                for half in range(2):
                    at = BLOCK * j + half * HALF
                    e = jnp.exp2(sb[at : at + HALF, :] * EXP2_SCALE - sh)
                    total = total + jnp.sum(e, axis=0, keepdims=True)
                    eb[hh, BLOCK + at : BLOCK + at + HALF, :] = e.astype(BF16)
            rl[hh] = 1.0 / total
            fades[hh] = fade
            return 0

        lax.fori_loop(0, GROUP, one_head, 0)

    def values_far(g):
        w_ = win[g]
        vt[1] = w_[1][col1].T
        vt[2] = w_[1][col2].T

        def one_head(r, _):
            hh = g * GROUP + r
            hcols = pl.ds(pl.multiple_of(hh * HD, HD), HD)
            out = ot[hcols, :] * fades[hh]
            out = out + nn(vt[1], eb[hh, BLOCK : 2 * BLOCK, :]) + nn(vt[2], eb[hh, 2 * BLOCK :, :])
            out = out * rl[hh]
            ot[hcols, :] = out
            ob[:, hcols] = out.T.astype(BF16)
            return 0

        lax.fori_loop(0, GROUP, one_head, 0, unroll=2)

    q_in.wait()
    for g in range(KV):
        forward_near(g)
    for g in range(KV):
        arrived(g, 0)
        scores_far(g)
    def project(block, cut, put, rows=slice(None)):
        def step(i, _):
            n0 = pl.multiple_of(i * 256, 256)
            cols = pl.ds(pl.multiple_of(block * WIDTH + cut * CUT + n0, 256), 256)
            put(pl.ds(n0, 256), nn(ob[:, rows], wv[rows, cols]))
            return 0

        lax.fori_loop(0, CUT // 256, step, 0)

    def hold(ref, cut):
        def put(cols, val):
            ref[cut, :, cols] = val

        return put

    early = slice(0, GROUP * HD)
    late = slice(GROUP * HD, WIDTH)
    arrived(0, 1)
    values_far(0)
    for j in range(CUTS):
        project(diagonal, j, hold(pdiag, j), early)
        project(other_chip, j, hold(pown, j), early)
    arrived(1, 1)
    values_far(1)

    def to_core(slot, cut):
        def put(cols, val):
            pcs[slot, cut, :, cols] = (val + pdiag[cut, :, cols] if slot == 0 else val).astype(BF16)

        return put

    def to_chip(cut):
        def put(cols, val):
            pxs[cut, :, cols] = (val + pown[cut, :, cols] + pcr[0, cut, :, cols].astype(F32)).astype(BF16)

        return put

    def keep(cut):
        def put(cols, val):
            pown[cut, :, cols] = val

        return put

    p_core = [
        [remote(pcs.at[i, j], pcr.at[i, j], pcss.at[i, j], pcrs.at[i, j], ctx, other_core) for j in range(CUTS)]
        for i in range(2)
    ]
    p_chip = [remote(pxs.at[j], pxr.at[j], pxss.at[j], pxrs.at[j], ctx, other_chip) for j in range(CUTS)]
    project(diagonal, 0, to_core(0, 0), late)
    p_core[0][0].start()
    project(diagonal, 1, to_core(0, 1), late)
    p_core[0][1].start()
    for j in range(CUTS):
        p_core[0][j].wait_recv()
        project(other_chip, j, to_chip(j), late)
        p_chip[j].start()
        if j == 0:
            for i in range(OG_CUTS):
                og_chip[i].wait_recv()
                og_pass[i].start()
    def grad_rest(g):
        steps = GROUP * HD // 256
        grad_block(other_chip, False, g * steps, (g + 1) * steps)
        if g == 0:
            for i in range(OG_CUTS):
                og_pass[i].wait_recv()
        grad_block(diagonal, False, g * steps, (g + 1) * steps)

    def back_tile(g, slot, w_, col, part, hh, q, do, rd, span):
        keys_at = slice(part * HALF, (part + 1) * HALF)
        e = eb[hh, slot * BLOCK + part * HALF : slot * BLOCK + (part + 1) * HALF, span]
        v = own[g, 1, keys_at] if slot == 0 else w_[1][col, keys_at]
        dp = nn(v, do)
        dsv = (e.astype(F32) * (dp - rd)).astype(BF16)
        acc[g, 0, slot, keys_at] += nn(dsv, q)
        return nn(kt[slot, :, keys_at], dsv)

    def value_far(g):
        for r in range(GROUP):
            hh = g * GROUP + r
            hcols = slice(hh * HD, (hh + 1) * HD)
            do32 = dot_[hcols, :] * rl[hh]
            do = do32.astype(BF16)
            rdb[hh] = jnp.sum(do32 * ot[hcols, :], axis=0, keepdims=True)
            dob[hcols, :] = do
            for slot in (1, 2):
                part = nt(eb[hh, slot * BLOCK : (slot + 1) * BLOCK, :], do)
                acc[g, 1, slot] = part if r == 0 else acc[g, 1, slot] + part

    def backward_far(g):
        w_ = win[g]
        kt[1] = w_[0][col1].T
        kt[2] = w_[0][col2].T
        acc[g, 0] = jnp.zeros(acc.shape[2:], F32)

        def one_head(r, _):
            hh = g * GROUP + r
            hcols = pl.ds(pl.multiple_of(hh * HD, HD), HD)
            q = qv[:, hcols]
            do = dob[hcols, :]
            rd = rdb[hh]
            dqt = jnp.zeros((HD, BLOCK), F32)
            for slot, col in ((1, col1), (2, col2)):
                for part in range(2):
                    dqt = dqt + back_tile(g, slot, w_, col, part, hh, q, do, rd, slice(None))
            dot_[hcols, :] = dqt
            return 0

        lax.fori_loop(0, GROUP, one_head, 0, unroll=GROUP)

    def backward_near(g):
        kt[0] = own[g, 0].T
        acc[g, 1, 0] = jnp.zeros((BLOCK, HD), F32)

        def one_head(r, _):
            hh = g * GROUP + r
            hcols = pl.ds(pl.multiple_of(hh * HD, HD), HD)
            q = qv[:, hcols]
            do = (dob[hcols, :].astype(F32) * fades[hh]).astype(BF16)
            rd = rdb[hh] * fades[hh]
            acc[g, 1, 0, :HALF] += nt(eb[hh, :HALF, :], do)
            acc[g, 1, 0, HALF:] += nt(eb[hh, HALF:BLOCK, HALF:], do[:, HALF:])
            dqt = dot_[hcols, :] + back_tile(g, 0, None, None, 0, hh, q, do, rd, slice(None))
            late = back_tile(g, 0, None, None, 1, hh, q[HALF:], do[:, HALF:], rd[:, HALF:], slice(HALF, BLOCK))
            dqt = jnp.concatenate([dqt[:, :HALF], dqt[:, HALF:] + late], axis=1)
            dqv[:, hcols] = (dqt * SCALE).T.astype(BF16)
            return 0

        lax.fori_loop(0, GROUP, one_head, 0, unroll=GROUP)

    give = [
        [
            [
                remote(
                    gs[g].at[lax.rem(y + ROW - k, ROW), part], gr[g].at[k - 1, part],
                    bds.at[g, part, k - 1], bdr.at[g, part, k - 1],
                    row_start + lax.rem(y + ROW - k, ROW), head,
                )
                for k in (1, 2, 3)
            ]
            for part in range(2)
        ]
        for g in range(KV)
    ]
    give_back = [
        [
            remote(gxs.at[g, part], gxr.at[g, part], bxs.at[g, part], bxr.at[g, part], preceding, head)
            for part in range(2)
        ]
        for g in range(KV)
    ]
    factors = (SCALE, 1.0)

    def send_grads(g, part):
        one = acc[g, part, 1] * factors[part]
        two = acc[g, part, 2] * factors[part]
        for c in range(ROW):
            gs[g][c, part] = (jnp.where(col1 == c, one, 0.0) + jnp.where(col2 == c, two, 0.0)).astype(BF16)
        for k in (1, 3, 2):
            give[g][part][k - 1].start()

    def sum_grads(g, part):
        for k in (1, 2, 3):
            give[g][part][k - 1].wait_recv()
        mine = None
        back = gs[g][y, part].astype(F32)
        for k in (1, 2, 3):
            came = gr[g][k - 1, part].astype(F32)
            inside = y + k < ROW
            kept = jnp.where(inside, came, 0.0)
            mine = kept if mine is None else mine + kept
            back = back + jnp.where(inside, 0.0, came)
        gxs[g, part] = back.astype(BF16)
        give_back[g][part].start()
        acc[g, part, 1] = mine

    outs = []

    def finish_grads(g, part):
        give_back[g][part].wait_recv()
        total = acc[g, part, 0] * factors[part] + acc[g, part, 1] + gxr[g, part].astype(F32)
        dkv_out[g, part] = total.astype(BF16)
        ref = (dk_hbm, dv_hbm)[part]
        cp = pltpu.make_async_copy(dkv_out.at[g, part], ref.at[:, pl.ds(g * HD, HD)], osem.at[2 * g + part])
        cp.start()
        outs.append(cp)

    for g in range(KV):
        grad_rest(g)
        value_far(g)
        send_grads(g, 1)
    for g in range(KV):
        backward_far(g)
        send_grads(g, 0)
    sum_grads(0, 1)
    backward_near(0)
    sum_grads(1, 1)
    backward_near(1)
    cp = pltpu.make_async_copy(dqv, dq_hbm, osem.at[4])
    cp.start()
    outs.append(cp)
    sum_grads(0, 0)
    for j in range(CUTS):
        project(other_core, j, to_core(1, j))
        p_core[1][j].start()
    for j in range(CUTS):
        project(head, j, keep(j))
    sum_grads(1, 0)
    for j in range(CUTS):
        p_core[1][j].wait_recv()
        p_chip[j].wait()
        pxs[j] = (pown[j] + pcr[1, j].astype(F32) + pxr[j].astype(F32)).astype(BF16)
        cp = pltpu.make_async_copy(pxs.at[j], proj_hbm.at[:, pl.ds(j * CUT, CUT)], osem.at[5 + j])
        cp.start()
        outs.append(cp)
    for g, part in ((0, 1), (1, 1), (0, 0), (1, 0)):
        finish_grads(g, part)

    og_core.wait_send()
    for i in range(OG_CUTS):
        og_chip[i].wait_send()
        og_pass[i].wait_send()
    for i in range(2):
        for j in range(CUTS):
            p_core[i][j].wait_send()
    for g in range(KV):
        for part in range(2):
            cross[g, part].wait_send()
            for k in (1, 2, 3):
                serve_own[g, part, k].wait_send()
            give_back[g][part].wait_send()
            for k in (1, 2, 3):
                give[g][part][k - 1].wait_send()
    for cp in outs:
        cp.wait()


def mover(*refs):
    ins, outs, held, sems = refs[:4], refs[4:8], refs[8:12], refs[12]
    copies = []
    for i, (n, first, rows) in enumerate(MOVES):
        at = pl.ds(first, rows)
        copies.append(
            (
                pltpu.make_async_copy(ins[n].at[at], held[n].at[at], sems.at[0, i]),
                pltpu.make_async_copy(held[n].at[at], outs[n].at[at], sems.at[1, i]),
            )
        )
    for come, _ in copies:
        come.start()
    for come, go in copies:
        come.wait()
        go.start()
    for _, go in copies:
        go.wait()


def local(queries, keys, values, selected, out_weight, out_grad):
    vm = pltpu.VMEM
    dma = pltpu.SemaphoreType.DMA
    anyspec = pl.BlockSpec(memory_space=pl.ANY)
    shapes = (
        jax.ShapeDtypeStruct((BLOCK, WIDTH), BF16),
        jax.ShapeDtypeStruct((BLOCK, WIDTH), BF16),
        jax.ShapeDtypeStruct((BLOCK, KV * HD), BF16),
        jax.ShapeDtypeStruct((BLOCK, KV * HD), BF16),
    )
    results = pl.pallas_call(
        kernel,
        out_shape=shapes,
        in_specs=[pl.BlockSpec(memory_space=pltpu.SMEM)] + [anyspec] * 5,
        out_specs=(anyspec,) * 4,
        scratch_shapes=[
            vm((KV, 2, BLOCK, HD), BF16),
            vm((ROW, BLOCK, HD), BF16),
            vm((ROW, BLOCK, HD), BF16),
            vm((ROW, BLOCK, HD), BF16),
            vm((ROW, BLOCK, HD), BF16),
            vm((3, HD, BLOCK), BF16),
            vm((3, HD, BLOCK), BF16),
            vm((BLOCK, WIDTH), BF16),
            vm((WIDTH, 4 * WIDTH), BF16),
            vm((4, BLOCK, WIDTH), BF16),
            vm((WIDTH, BLOCK), F32),
            vm((WIDTH, BLOCK), F32),
            vm((BLOCK, WIDTH), BF16),
            vm((KV * GROUP, 1, BLOCK), F32),
            vm((KV * GROUP, 3 * BLOCK, BLOCK), BF16),
            vm((2 * BLOCK, BLOCK), F32),
            vm((KV, 2, 3, BLOCK, HD), F32),
            vm((ROW, 2, BLOCK, HD), BF16),
            vm((ROW, 2, BLOCK, HD), BF16),
            vm((3, 2, BLOCK, HD), BF16),
            vm((3, 2, BLOCK, HD), BF16),
            vm((KV, 2, BLOCK, HD), BF16),
            vm((KV, 2, BLOCK, HD), BF16),
            vm((2, CUTS, BLOCK, CUT), BF16),
            vm((2, CUTS, BLOCK, CUT), BF16),
            vm((CUTS, BLOCK, CUT), BF16),
            vm((CUTS, BLOCK, CUT), BF16),
            vm((CUTS, BLOCK, CUT), F32),
            vm((BLOCK, WIDTH), BF16),
            vm((KV, 2, BLOCK, HD), BF16),
            vm((WIDTH, BLOCK), BF16),
            vm((KV * GROUP, 1, BLOCK), F32),
            vm((KV * GROUP, 1, BLOCK), F32),
            vm((KV * GROUP, 1, BLOCK), F32),
            vm((KV * GROUP, 1, BLOCK), F32),
            vm((CUTS, BLOCK, CUT), F32),
            dma((7,)), dma((5 + CUTS,)),
            dma((KV, 2)), dma((KV, 2)), dma((KV, 2, 3)), dma((KV, 2, 3)),
            dma((1,)), dma((1,)), dma((OG_CUTS,)), dma((OG_CUTS,)), dma((OG_CUTS,)), dma((OG_CUTS,)),
            dma((2, CUTS)), dma((2, CUTS)), dma((CUTS,)), dma((CUTS,)),
            dma((KV, 2, 3)), dma((KV, 2, 3)), dma((KV, 2)), dma((KV, 2)),
        ],
        compiler_params=pltpu.CompilerParams(
            collective_id=0, has_side_effects=True, vmem_limit_bytes=63 * 1024 * 1024
        ),
        cost_estimate=pl.CostEstimate(flops=18 * 10**9, bytes_accessed=16 * 2**20, transcendentals=6 * 10**6),
        name="layer",
    )(selected, queries, keys, values, out_weight, out_grad)
    return pl.pallas_call(
        mover,
        out_shape=shapes,
        in_specs=[anyspec] * 4,
        out_specs=(anyspec,) * 4,
        scratch_shapes=[vm(x.shape, x.dtype) for x in shapes] + [dma((2, len(MOVES)))],
        compiler_params=pltpu.CompilerParams(vmem_limit_bytes=60 * 1024 * 1024),
        name="move",
    )(*results)


def solution(mesh):
    placed = (
        P("ctx", "head"),
        P("ctx", "head"),
        P("ctx", "head"),
        P("ctx", None),
        P("head", None),
        P("ctx", "head"),
    )
    return jax.shard_map(
        local,
        mesh=mesh,
        in_specs=placed,
        out_specs=(P("ctx", "head"), P("ctx", "head"), P("ctx", "head"), P("ctx", "head")),
        check_vma=False,
    )
```
